128 devices in a mesh: node: 64 (over x_lo, z, y, core), feat: 2 (over x_hi).
Axes of the slice: x: 4 (x_hi: 2, x_lo: 2; x = x_hi * 2 + x_lo), y: 4, z: 4, core: 2. Of those that a mesh axis runs over, the one named last changes fastest.
Arguments:
- node_feats: bfloat16 [65536, 1024], P('node', 'feat'), may hold values from -6 to 6
- edge_tiles: bfloat16 [1280, 128, 128], P('node'), may hold values from 0.001953125 to 0.078125
- slot_row: int32 [64, 20], P('node'), may hold values from 0 to 7
- slot_col: int32 [64, 20], P('node'), may hold values from 0 to 7
- slot_tile: int32 [64, 20], P('node'), may hold values from 0 to 19, each once within a row
- slot_count: int32 [64, 5], P('node'), may hold values from 1 to 4, as said below
- w_self: bfloat16 [1024, 1024], P('feat'), may hold values from -0.1875 to 0.1875
- w_neigh: bfloat16 [1024, 1024], P('feat'), may hold values from -0.1875 to 0.1875
- bias: float32 [1024], P('feat'), may hold values from -3 to 3
- cotangent: bfloat16 [65536, 1024], P('node', 'feat'), may hold values from -6 to 6
Outputs:
- hidden_out: bfloat16 [65536, 1024], P('node', 'feat')
- grad_nodes: bfloat16 [65536, 1024], P('node', 'feat')
- grad_self: float32 [1024, 1024], P('feat')
- grad_neigh: float32 [1024, 1024], P('feat')
- grad_bias: float32 [1024], P('feat')
The draws below stay inside these ranges and needn't reach their ends.
Inputs may be any that keep to these rules, and one draw needn't show every extreme that they name: `slot_count`: 4 is reached on some device. `slot_tile`: each device's row names each of its tiles once.
All inputs are finite; a program needn't handle non-finite values.
Results may differ from the reference program's by a relative error of at most 0.007.
Values may be sent and summed in bfloat16 or wider, within the bound.
No kernel may reach another device: no remote copies, remote signals or barrier semaphores. Data moves between devices by JAX's collectives and lax.ppermute only.
A program may use at most 128 MiB of HBM per device.

```python
import math
import jax
import jax.numpy as jnp
from jax import lax

F = 1024
H = 1024
BLOCK = 128
REACH = 2
PAIR_MAX = 4
SPAN = 5
RB = 8
TILES_DEV = 20
TILES_ALL = 1280
NODES = 65536
N_NODE = 64


def draw_slot_count(key, part):
    key = jax.random.fold_in(key, 7)
    key_cap, key_top, key_count, key_full = jax.random.split(key, 4)
    capacity = jax.random.randint(key_cap, (N_NODE,), 1, PAIR_MAX + 1)
    busiest = jax.random.randint(key_top, (), 0, N_NODE)
    capacity = jnp.where(jnp.arange(N_NODE) == busiest, PAIR_MAX, capacity)
    lowest = (capacity + 1) // 2
    live_count = jax.random.randint(key_count, (N_NODE, SPAN), lowest[:, None], capacity[:, None] + 1)
    fullest = jax.random.randint(key_full, (N_NODE,), 0, SPAN)
    live_count = jnp.where(jnp.arange(SPAN)[None, :] == fullest[:, None], capacity[:, None], live_count)
    return live_count.astype(jnp.int32)


def set_ends(entries, stream_key, low, top_value):
    shape = entries.shape
    index_at = [jax.random.randint(jax.random.fold_in(stream_key, axis), (), 0, shape[axis]) for axis in range(len(shape))]
    entries = entries.at[tuple(index_at)].set(low)
    longest = shape.index(max(shape))
    index_at[longest] = (index_at[longest] + 1) % shape[longest]
    return entries.at[tuple(index_at)].set(top_value)


def block_levels(stream_key, shape, cuts, least, top_value):
    loudness = 1.0
    for dim, parts in cuts:
        heights = jax.random.uniform(jax.random.fold_in(jax.random.fold_in(stream_key, 6), dim), (parts,), jnp.float32, least / len(cuts), top_value / len(cuts))
        loudness = loudness * jnp.repeat(jnp.exp(heights), shape[dim] // parts).reshape((-1,) + (1,) * (len(shape) - 1 - dim))
    return loudness


def bell_draw(rng, extent, spread, reach, shards=(), kind=jnp.bfloat16):
    loudness = block_levels(rng, extent, shards, -0.22, 0.18) if shards else 1.0
    array = jax.random.normal(rng, extent, jnp.float32) * spread * loudness
    return jnp.minimum(jnp.maximum(array, -reach), reach).astype(kind)


def setup_inputs(seed: int = 0) -> dict:
    splits = jax.random.split(jax.random.key(seed), 11)
    node_feats = bell_draw(splits[0], (NODES, F), 1.0, 6.0, ((0, 64), (1, 2)))
    edge_tiles = jnp.clip(jnp.exp(math.log(0.078125) - 3.6888795 * jax.random.uniform(splits[1], (TILES_ALL, BLOCK, BLOCK), jnp.float32) ** block_levels(splits[1], (TILES_ALL, BLOCK, BLOCK), ((0, 64),), -0.2, 0.2)), 0.001953125, 0.078125).astype(jnp.bfloat16)
    slot_row = set_ends(jax.random.randint(splits[2], (N_NODE, TILES_DEV), 0, RB), jax.random.fold_in(splits[2], 1), 0, RB - 1).astype(jnp.int32)
    slot_col = set_ends(jax.random.randint(splits[3], (N_NODE, TILES_DEV), 0, RB), jax.random.fold_in(splits[3], 1), 0, RB - 1).astype(jnp.int32)
    slot_tile = jax.vmap(lambda own: jax.random.permutation(own, TILES_DEV))(jax.random.split(splits[4], N_NODE)).reshape((N_NODE, TILES_DEV)).astype(jnp.int32)
    slot_count = draw_slot_count(jax.random.fold_in(splits[10], 71), 0)
    w_self = bell_draw(splits[6], (F, H), F ** -0.5, 0.1875, ((0, 2),))
    w_neigh = bell_draw(splits[7], (F, H), F ** -0.5, 0.1875, ((0, 2),))
    bias = bell_draw(splits[8], (H,), 0.5, 3.0, ((0, 2),), jnp.float32)
    cotangent = bell_draw(splits[9], (NODES, H), 1.0, 6.0, ((0, 64), (1, 2)))
    return dict(node_feats=node_feats, edge_tiles=edge_tiles, slot_row=slot_row, slot_col=slot_col, slot_tile=slot_tile, slot_count=slot_count, w_self=w_self, w_neigh=w_neigh, bias=bias, cotangent=cotangent)


def tile_tables(edge_tiles, slot_tile, slot_count):
    slot_index = jnp.arange(TILES_DEV, dtype=jnp.int32)
    offsets = (slot_index // PAIR_MAX).astype(jnp.int32)
    slot_live = (slot_index % PAIR_MAX)[None, :] < slot_count[:, offsets]
    devices = jnp.arange(N_NODE, dtype=jnp.int32)
    sources = ((devices[:, None] + offsets[None, :] - REACH) % N_NODE).astype(jnp.int32)
    stacked = edge_tiles.reshape(N_NODE, TILES_DEV, BLOCK, BLOCK)
    chosen = jnp.take_along_axis(stacked, slot_tile.astype(jnp.int32)[:, :, None, None], axis=1)
    weights = chosen.astype(jnp.float32) * slot_live[:, :, None, None].astype(jnp.float32)
    return (sources, weights)

def apply_graph(field, sources, slot_row, slot_col, weights):
    columns = field.shape[1]
    blocks = field.reshape(N_NODE, RB, BLOCK, columns)
    levels = jnp.arange(RB, dtype=jnp.int32)

    def one_device(items):
        source_ids, row_ids, column_ids, tile_values = items
        picked = blocks[source_ids, column_ids]
        product = jnp.einsum('tab,tbw->taw', tile_values, picked, precision=lax.Precision.HIGHEST)
        onehot = (row_ids[None, :] == levels[:, None]).astype(field.dtype)
        return jnp.einsum('rt,taw->raw', onehot, product, precision=lax.Precision.HIGHEST)
    result = lax.map(one_device, (sources, slot_row, slot_col, weights))
    return result.reshape(N_NODE * RB * BLOCK, columns)

def reference(node_feats, edge_tiles, slot_row, slot_col, slot_tile, slot_count, w_self, w_neigh, bias, cotangent):
    sources, weights = tile_tables(edge_tiles, slot_tile, slot_count)
    features = node_feats.astype(jnp.float32)

    def linear(field):
        return apply_graph(field, sources, slot_row, slot_col, weights)
    aggregate = linear(features).astype(jnp.bfloat16)
    preact = jnp.dot(aggregate, w_neigh, preferred_element_type=jnp.float32) + jnp.dot(node_feats, w_self, preferred_element_type=jnp.float32) + bias.astype(jnp.float32)
    sigma = jax.nn.sigmoid(preact)
    hidden_out = (preact * sigma).astype(jnp.bfloat16)
    delta = (cotangent.astype(jnp.float32) * sigma * (1.0 + preact * (1.0 - sigma))).astype(jnp.bfloat16)
    scale = float(NODES) ** (-0.5)
    grad_neigh = jnp.dot(aggregate.T, delta, preferred_element_type=jnp.float32) * scale
    grad_self = jnp.dot(node_feats.T, delta, preferred_element_type=jnp.float32) * scale
    grad_bias = lax.optimization_barrier(jnp.sum(delta.astype(jnp.float32), axis=0)) * scale
    delta_agg = jnp.dot(delta, w_neigh.T, preferred_element_type=jnp.float32).astype(jnp.bfloat16)
    outcome, pullback = jax.vjp(linear, features)
    back, = pullback(delta_agg.astype(outcome.dtype))
    grad_nodes = (jnp.dot(delta, w_self.T, preferred_element_type=jnp.float32) + back).astype(jnp.bfloat16)
    return (hidden_out, grad_nodes, grad_self, grad_neigh, grad_bias)
```

```python
import jax
import jax.numpy as jnp
from jax import lax
from jax.experimental import pallas as pl
from jax.experimental.pallas import tpu as pltpu
from jax.sharding import Mesh, PartitionSpec as P

REACH = 2
PAIR_MAX = 4
BLOCK = 128
OFFSETS = (0, 1, 3, 4)
NODE = ("xl", "z", "y", "c")
CHIPS = ("xl", "z", "y")
VMEM = pl.BlockSpec(memory_space=pltpu.VMEM)
SMEM = pl.BlockSpec(memory_space=pltpu.SMEM)
BF = jnp.bfloat16
F32 = jnp.float32
MIB = 1 << 20


def dot(a, b, dims=((1,), (0,))):
    return lax.dot_general(a, b, (dims, ((), ())), preferred_element_type=F32)


def shift(block, distance):
    count = lax.axis_size(NODE)
    return lax.ppermute(block, NODE, [(i, (i + distance) % count) for i in range(count)])


def swap(block, axis):
    return lax.ppermute(block, axis, [(0, 1), (1, 0)])


def call(kernel, outs, in_specs, scratch=(), flops=0, moved=0, vmem=24):
    return pl.pallas_call(
        kernel,
        out_shape=outs,
        in_specs=in_specs,
        out_specs=[VMEM] * len(outs),
        scratch_shapes=list(scratch),
        compiler_params=pltpu.CompilerParams(vmem_limit_bytes=vmem * MIB),
        cost_estimate=pl.CostEstimate(flops=flops, bytes_accessed=moved, transcendentals=0),
    )


def shape(dims, kind):
    return jax.ShapeDtypeStruct(dims, kind)


def pick_kernel(cols, x, *outs):
    for i, out in enumerate(outs):
        for s in range(PAIR_MAX):
            out[s] = x[cols[i, s]]


def aggregate_kernel(place, row, col, tile, count, x, h0, h1, h3, h4, tiles, w_neigh, w_self, agg, send0, send1, acc):
    halos = (h0, h1, None, h3, h4)
    acc[...] = jnp.zeros_like(acc)
    for j in range(5 * PAIR_MAX):
        k, s = divmod(j, PAIR_MAX)

        @pl.when(s < count[0, k])
        def _():
            block = x[col[0, j]] if k == REACH else halos[k][s]
            acc[row[0, j]] += dot(tiles[tile[0, j]], block)

    half = send0.shape[1]
    other = (1 - place[0]) * (2 * half)

    def rows(r, _):
        mine = acc[r].astype(BF)
        agg[r] = mine
        for c, send in enumerate((send0, send1)):
            cols = pl.ds(pl.multiple_of(other + c * half, 128), half)
            send[pl.ds(pl.multiple_of(r * BLOCK, BLOCK), BLOCK), :] = (
                dot(mine, w_neigh[:, cols]) + dot(x[r], w_self[:, cols])
            ).astype(BF)
        return 0

    lax.fori_loop(0, x.shape[0], rows, 0)


def own_kernel(place, agg, x, w_neigh, w_self, bias, out):
    width = out.shape[1]
    cols = pl.ds(pl.multiple_of(place[0] * width, 128), width)
    out[...] = dot(agg[...], w_neigh[:, cols]) + dot(x[...], w_self[:, cols]) + bias[...]


def act_kernel(own, recv, cot, *rest):
    hidden, delta, sums = rest[-3:]
    pre = own[...] + recv[...].astype(F32)
    sigma = jax.nn.sigmoid(pre)
    hidden[...] = (pre * sigma).astype(BF)
    d = (cot[...].astype(F32) * sigma * (1.0 + pre * (1.0 - sigma))).astype(BF)
    delta[...] = d

    @pl.when(pl.program_id(0) == 0)
    def _():
        sums[...] = jnp.zeros_like(sums)

    sums[...] += jnp.sum(d.astype(F32).reshape(-1, 8, d.shape[1]), axis=0)


def weight_kernel(place, agg, x, d0, d1, send, keep):
    half = d0.shape[1]
    core = place[1]

    def cols(i, _):
        at = pl.ds(pl.multiple_of(i * BLOCK, BLOCK), BLOCK)
        for c, d in enumerate((d0, d1)):
            neigh = dot(agg[:, at], d[...], ((0,), (0,)))
            own = dot(x[:, at], d[...], ((0,), (0,)))
            first = core == 0
            span = slice(c * half, (c + 1) * half)
            send[at, span] = jnp.where(first, own, neigh).astype(BF)
            keep[at, span] = jnp.where(first, neigh, own)
        return 0

    lax.fori_loop(0, agg.shape[1] // BLOCK, cols, 0)


def back_kernel(place, row, col, tile, count, own0, own1, far0, far1, tiles, w_neigh, w_self, o0, o1, o3, o4, base, dagg):
    outs = (o0, o1, None, o3, o4)
    half = own0.shape[1]
    mine, other = place[0] * (2 * half), (1 - place[0]) * (2 * half)

    def rows(r, _):
        at = pl.ds(pl.multiple_of(r * BLOCK, BLOCK), BLOCK)
        to_neigh = jnp.zeros((BLOCK, dagg.shape[2]), F32)
        to_self = jnp.zeros((BLOCK, dagg.shape[2]), F32)
        for d, start in ((own0, mine), (own1, mine + half), (far0, other), (far1, other + half)):
            cols = pl.ds(pl.multiple_of(start, 128), half)
            to_neigh += dot(d[at, :], w_neigh[:, cols], ((1,), (1,)))
            to_self += dot(d[at, :], w_self[:, cols], ((1,), (1,)))
        dagg[r] = to_neigh.astype(BF)
        base[r] = to_self
        return 0

    lax.fori_loop(0, base.shape[0], rows, 0)
    for j in range(5 * PAIR_MAX):
        k, s = divmod(j, PAIR_MAX)
        weight = tiles[tile[0, j]]
        live = s < count[0, k]
        if k == REACH:

            @pl.when(live)
            def _():
                base[col[0, j]] += dot(weight, dagg[row[0, j]], ((0,), (0,)))
        else:

            @pl.when(live)
            def _():
                outs[k][s] = dot(weight, dagg[row[0, j]], ((0,), (0,))).astype(BF)

            @pl.when(jnp.logical_not(live))
            def _():
                outs[k][s] = jnp.zeros(outs[k].shape[1:], BF)


def place_kernel(cols, base, r0, r1, r3, r4, out, acc):
    acc[...] = base[...]
    for i, r in enumerate((r0, r1, r3, r4)):
        for s in range(PAIR_MAX):
            acc[cols[i, s]] += r[s].astype(F32)
    out[...] = acc[...].astype(BF)


def assemble_kernel(place, own_mine, own_swap, far_mine, far_swap, neigh, self_):
    width = own_mine.shape[1]
    core = place[1] == 0
    for a, b, side in ((own_mine, own_swap, place[0]), (far_mine, far_swap, 1 - place[0])):
        cols = pl.ds(pl.multiple_of(side * width, 128), width)
        neigh[:, cols] = jnp.where(core, a[...], b[...]).astype(F32)
        self_[:, cols] = jnp.where(core, b[...], a[...]).astype(F32)


def reduce_nodes(parts, scale):
    moved = lax.all_to_all(parts, CHIPS, 0, 0)
    total = jnp.sum(moved.astype(F32), axis=0) * scale
    return total


def spread(total):
    chips = lax.axis_size(CHIPS)
    whole = lax.all_to_all(jnp.broadcast_to(total.astype(BF)[None], (chips, *total.shape)), CHIPS, 0, 0)
    return whole.reshape(chips * total.shape[0], total.shape[1])


def on_device(node_feats, edge_tiles, slot_row, slot_col, slot_tile, slot_count, w_self, w_neigh, bias, cotangent):
    nodes, width = node_feats.shape
    blocks = nodes // BLOCK
    half = width // 2
    chips = lax.axis_size(CHIPS)
    piece = width // chips
    place = jnp.stack([lax.axis_index("f"), lax.axis_index("c")]).astype(jnp.int32)
    scale = float(nodes * lax.axis_size(NODE)) ** (-0.5)
    x = node_feats.reshape(blocks, BLOCK, width)
    lists = (place, slot_row, slot_col, slot_tile, slot_count)

    wanted = jnp.concatenate(
        [shift(slot_col[:, k * PAIR_MAX : (k + 1) * PAIR_MAX], k - REACH) for k in OFFSETS], axis=0
    )
    slab = shape((PAIR_MAX, BLOCK, width), BF)
    picked = call(pick_kernel, [slab] * 4, [SMEM, VMEM], moved=3 * MIB)(wanted, x)
    halos = [shift(p, REACH - k) for k, p in zip(OFFSETS, picked)]

    agg, send0, send1 = call(
        aggregate_kernel,
        [shape((blocks, BLOCK, width), BF)] + [shape((nodes, half), BF)] * 2,
        [SMEM] * 5 + [VMEM] * 8,
        [pltpu.VMEM((blocks, BLOCK, width), F32)],
        flops=2 * 10**9,
        moved=8 * MIB,
    )(*lists, x, *halos, edge_tiles, w_neigh, w_self)
    recv = [swap(send0, "f"), swap(send1, "f")]
    aggregate = agg.reshape(nodes, width)

    tall = nodes // 4
    own = pl.pallas_call(
        own_kernel,
        grid=(4,),
        out_shape=shape((nodes, width), F32),
        in_specs=[
            SMEM,
            pl.BlockSpec((tall, width), lambda i: (i, 0)),
            pl.BlockSpec((tall, width), lambda i: (i, 0)),
            pl.BlockSpec(w_neigh.shape, lambda i: (0, 0)),
            pl.BlockSpec(w_self.shape, lambda i: (0, 0)),
            pl.BlockSpec((1, width), lambda i: (0, 0)),
        ],
        out_specs=pl.BlockSpec((tall, width), lambda i: (i, 0)),
        compiler_params=pltpu.CompilerParams(vmem_limit_bytes=24 * MIB),
        cost_estimate=pl.CostEstimate(flops=10**9, bytes_accessed=6 * MIB, transcendentals=0),
    )(place, aggregate, node_feats, w_neigh, w_self, bias.reshape(1, width))

    hidden = None
    delta, sums = [], []
    for c in range(2):
        column = pl.BlockSpec((tall, half), lambda i, c=c: (i, c))
        alone = pl.BlockSpec((tall, half), lambda i: (i, 0))
        extra = [] if c == 0 else [hidden]
        hidden, d, s = pl.pallas_call(
            act_kernel,
            grid=(4,),
            out_shape=[shape((nodes, width), BF), shape((nodes, half), BF), shape((8, half), F32)],
            in_specs=[column, alone, column] + [pl.BlockSpec(memory_space=pl.ANY)] * len(extra),
            out_specs=[column, alone, pl.BlockSpec((8, half), lambda i: (0, 0))],
            input_output_aliases={3: 0} if extra else {},
            compiler_params=pltpu.CompilerParams(vmem_limit_bytes=24 * MIB),
            cost_estimate=pl.CostEstimate(flops=10**7, bytes_accessed=3 * MIB, transcendentals=10**6),
        )(own, recv[c], cotangent, *extra)
        delta.append(d)
        sums.append(s)
    far = [swap(d, "f") for d in delta]

    def weights(d0, d1):
        return call(
            weight_kernel,
            [shape((width, width), BF), shape((width, width), F32)],
            [SMEM] + [VMEM] * 4,
            flops=10**9,
            moved=5 * MIB,
        )(place, aggregate, node_feats, d0, d1)

    def high_low(v):
        high = v.astype(BF)
        low = (v - high.astype(F32)).astype(BF)
        return jnp.concatenate([high, low, jnp.zeros((6, v.shape[1]), BF)], axis=0)

    bias_part = jnp.sum(jnp.concatenate(sums, axis=1), axis=0, keepdims=True)
    send, keep = weights(*delta)
    got, bias_got = swap(send, "c"), swap(bias_part, "c")
    parts = (keep + got.astype(F32)).astype(BF).reshape(chips, piece, width)
    bias_rows = jnp.broadcast_to(high_low(bias_part + bias_got)[None], (chips, 8, width))
    total = reduce_nodes(jnp.concatenate([parts, bias_rows], axis=1), scale)
    own_mine = spread(total[:piece])
    own_swap = swap(own_mine, "c")
    grad_bias = total[piece] + total[piece + 1]

    *outward, base = call(
        back_kernel,
        [slab] * 4 + [shape((blocks, BLOCK, width), F32)],
        [SMEM] * 5 + [VMEM] * 7,
        [pltpu.VMEM((blocks, BLOCK, width), BF)],
        flops=2 * 10**9,
        moved=10 * MIB,
    )(*lists, *delta, *far, edge_tiles, w_neigh, w_self)
    returned = [shift(o, k - REACH) for k, o in zip(OFFSETS, outward)]

    send, keep = weights(*far)
    parts = (keep + swap(send, "c").astype(F32)).astype(BF).reshape(chips, piece, width)
    far_mine = spread(reduce_nodes(parts, scale))
    far_swap = swap(far_mine, "c")

    grad_nodes = call(
        place_kernel,
        [shape((blocks, BLOCK, width), BF)],
        [SMEM] + [VMEM] * 5,
        [pltpu.VMEM((blocks, BLOCK, width), F32)],
        moved=5 * MIB,
    )(wanted, base, *returned)[0].reshape(nodes, width)

    grad_neigh, grad_self = call(
        assemble_kernel,
        [shape((width, 2 * width), F32)] * 2,
        [SMEM] + [VMEM] * 4,
        moved=6 * MIB,
    )(place, own_mine, own_swap, far_mine, far_swap)
    return hidden, grad_nodes, grad_self, grad_neigh, grad_bias


def solution(mesh):
    fine = Mesh(mesh.devices.reshape(2, 4, 4, 2, 2), (*NODE, "f"))
    placed = (
        P(NODE, "f"),
        P(NODE, None, None),
        P(NODE, None),
        P(NODE, None),
        P(NODE, None),
        P(NODE, None),
        P("f", None),
        P("f", None),
        P("f"),
        P(NODE, "f"),
    )
    return jax.shard_map(
        on_device,
        mesh=fine,
        in_specs=placed,
        out_specs=(P(NODE, "f"), P(NODE, "f"), P("f", None), P("f", None), P("f")),
        check_vma=False,
    )
```

```python
import jax
import jax.numpy as jnp
from jax import lax
from jax.experimental import pallas as pl
from jax.experimental.pallas import tpu as pltpu
from jax.sharding import Mesh, PartitionSpec as P

REACH = 2
PAIR_MAX = 4
BLOCK = 128
NODE = ("xl", "z", "y", "c")
CHIPS = ("xl", "z", "y")
PLANE = ("z", "y")
VMEM = pl.BlockSpec(memory_space=pltpu.VMEM)
SMEM = pl.BlockSpec(memory_space=pltpu.SMEM)
HBM = pl.BlockSpec(memory_space=pltpu.HBM)
ANY = pl.BlockSpec(memory_space=pl.ANY)
BF = jnp.bfloat16
F32 = jnp.float32
MIB = 1 << 20
ROLES = ((4, 0), (0, 4), (1, 3), (3, 1))
TALL = 256
COST = pl.CostEstimate(flops=10**4, bytes_accessed=10**4, transcendentals=0)


def dot(a, b, dims=((1,), (0,))):
    return lax.dot_general(a, b, (dims, ((), ())), preferred_element_type=F32)


def mirror(block, distance):
    count = lax.axis_size(NODE)
    return lax.ppermute(
        block, NODE, [(i, (i + (distance if i % 2 == 0 else -distance)) % count) for i in range(count)]
    )


def swap(block, axis):
    return lax.ppermute(block, axis, [(0, 1), (1, 0)])


def send_roles(blocks):
    ahead, behind, outer, sibling = blocks
    return [mirror(ahead, REACH), mirror(behind, -REACH), mirror(outer, -1), swap(sibling, "c")]


def shape(dims, kind):
    return jax.ShapeDtypeStruct(dims, kind)


def params(vmem):
    return pltpu.CompilerParams(vmem_limit_bytes=vmem * MIB)


def live(count, k, s):
    return s < count[0, k]


def pass_kernel(array, *rest):
    pass


def mark_kernel(*refs):
    refs[-1][...] = jnp.zeros_like(refs[-1])


def turn_kernel(x, w_neigh, w_self, tiles, x_t, neigh_t, self_t, tiles_t, token):
    x_t[...] = x[...].T
    neigh_t[...] = w_neigh[...].T
    self_t[...] = w_self[...].T
    for j in range(tiles.shape[0]):
        tiles_t[j] = tiles[j].T
    token[...] = jnp.zeros_like(token)


def early_kernel(row, col, tile, count, x, near, tiles, w_self, bias, after, acc, ahead, own, token):
    token[...] = jnp.zeros_like(token)
    core = lax.axis_index("c")
    acc[...] = jnp.zeros_like(acc)
    for k, source in ((REACH, x), (jnp.where(core == 0, 3, 1), near)):
        for s in range(PAIR_MAX):
            j = k * PAIR_MAX + s

            @pl.when(live(count, k, s))
            def _():
                acc[row[0, j]] += dot(tiles[tile[0, j]], source[col[0, j]])

    width = own.shape[1]
    side = lax.axis_index("f")
    rows = TALL
    for r in range(own.shape[0] // rows):
        at = slice(r * rows, (r + 1) * rows)
        mine = x[r * rows // BLOCK : (r + 1) * rows // BLOCK].reshape(rows, width)
        ahead[at, :] = dot(mine, w_self[:, pl.ds(pl.multiple_of((1 - side) * width, 128), width)])
        own[at, :] = dot(mine, w_self[:, pl.ds(pl.multiple_of(side * width, 128), width)]) + bias[...]


def aggregate_kernel(row, col, tile, count, ahead, passing, passed, acc0, part, tiles, w_neigh, agg, send0, send1, acc):
    core = lax.axis_index("c")
    acc[...] = acc0[...]
    for (k0, k1), source in zip(((0, 4), (4, 0), (1, 3)), (ahead, passing, passed)):
        k = jnp.where(core == 0, k0, k1)
        for s in range(PAIR_MAX):
            j = k * PAIR_MAX + s

            @pl.when(live(count, k, s))
            def _():
                acc[row[0, j]] += dot(tiles[tile[0, j]], source[col[0, j]])

    rows = acc.shape[0] * BLOCK // 2
    half = send0.shape[1]
    agg[...] = acc[...].astype(BF).reshape(agg.shape)
    other = (1 - lax.axis_index("f")) * (2 * half)
    for c, send in enumerate((send0, send1)):
        cols = pl.ds(pl.multiple_of(other + c * half, 128), half)
        span = slice(c * half, (c + 1) * half)
        for r in range(2):
            at = slice(r * rows, (r + 1) * rows)
            send[at, :] = (dot(agg[at, :], w_neigh[:, cols]) + part[at, span]).astype(BF)


def own_kernel(agg, own0, w_neigh, out, agg_t):
    width = out.shape[1]
    cols = pl.ds(pl.multiple_of(lax.axis_index("f") * width, 128), width)
    out[...] = dot(agg[...], w_neigh[:, cols]) + own0[...]
    agg_t[...] = agg[...].T


def act_kernel(own, recv, cot, *rest):
    hidden, delta, sums = rest[-3:]
    pre = own[...] + recv[...].astype(F32)
    sigma = jax.nn.sigmoid(pre)
    hidden[...] = (pre * sigma).astype(BF)
    d = (cot[...].astype(F32) * sigma * (1.0 + pre * (1.0 - sigma))).astype(BF)
    delta[...] = d

    @pl.when(pl.program_id(0) == 0)
    def _():
        sums[...] = jnp.zeros_like(sums)

    sums[...] += jnp.sum(d.astype(F32).reshape(-1, 8, d.shape[1]), axis=0)


def weight_kernel(agg_t, x_t, d, *rest):
    send, keep = rest[-2:]
    first = lax.axis_index("c") == 0
    neigh = dot(agg_t[...], d[...])
    own = dot(x_t[...], d[...])
    send[...] = jnp.where(first, own, neigh).astype(BF)
    keep[...] = jnp.where(first, neigh, own)


def weight_total_kernel(agg_t, x_t, d, moved, c0, c1, c2, c3, send, keep, total, token):
    token[...] = jnp.zeros_like(token)
    weight_kernel(agg_t, x_t, d, send, keep)
    total[...] = jnp.sum(moved[...].astype(F32), axis=0)


def bias_rows(sums):
    total = jnp.sum(sums, axis=0, keepdims=True)
    high = total.astype(BF)
    low = (total - high.astype(F32)).astype(BF)
    row = lax.broadcasted_iota(jnp.int32, (8, total.shape[1]), 0)
    return jnp.where(row == 0, high.astype(F32), jnp.where(row == 1, low.astype(F32), 0.0)).astype(BF)


def join_kernel(keep, got, *rest):
    out = rest[-1]
    pieces, tall, width = out.shape
    piece = keep.shape[0] // pieces
    both = (keep[...] + got[...].astype(F32)).astype(BF)
    out[:, :piece, :] = both.reshape(pieces, piece, width)
    if tall > piece:
        s0, s1, g0, g1 = rest[:-1]
        half = s0.shape[1]
        for c, (s, g) in enumerate(((s0, g0), (s1, g1))):
            rows = bias_rows(jnp.concatenate([s[...], g[...]], axis=0))
            out[:, piece:, c * half : (c + 1) * half] = jnp.broadcast_to(rows[None], (pieces, 8, half))


def spread_kernel(scale, a, b, moved, after, also, out, bias):
    piece = out.shape[1] // 2
    xl = lax.axis_index("xl")
    rows = pl.ds(pl.multiple_of(xl * piece, piece), piece)
    mine = (a[rows, :] + b[rows, :]) * scale
    far = jnp.sum(moved[...].astype(F32), axis=0) * scale
    out[:, :piece, :] = jnp.broadcast_to(mine.astype(BF)[None], (out.shape[0], *mine.shape))
    out[:, piece:, :] = jnp.broadcast_to(far.astype(BF)[None], (out.shape[0], *far.shape))
    bias[...] = jnp.sum((a[2 * piece :, :] + b[2 * piece :, :]) * scale, axis=0, keepdims=True)


def wide(own, far, turned, r, rows):
    side = lax.axis_index("f")
    width = own.shape[1]
    at = slice(r * rows, (r + 1) * rows)
    mine = turned[pl.ds(pl.multiple_of(side * width, 128), width), :]
    other = turned[pl.ds(pl.multiple_of((1 - side) * width, 128), width), :]
    return dot(own[at, :], mine) + dot(far[at, :], other)


def outward_kernel(
    row, tile, count, own, far, tiles, turned, after,
    o0, o1, o2, o3, dagg, token, ds, df, ts, wn, dg, built, sems, sent,
):
    token[...] = jnp.zeros_like(token)
    pieces = [(turned, wn), (own, ds), (far, df), (tiles, ts), (dg, dagg)]
    copies = [pltpu.make_async_copy(a, b, sems.at[i]) for i, (a, b) in enumerate(pieces)]
    for c in copies[:4]:
        c.start()
    for c in copies[:3]:
        c.wait()
    blocks = dg.shape[0]
    for r in range(2):
        total = wide(ds, df, wn, r, blocks * BLOCK // 2)
        dg[r * blocks // 2 : (r + 1) * blocks // 2] = total.astype(BF).reshape(blocks // 2, BLOCK, -1)
    copies[4].start()
    copies[3].wait()
    core = lax.axis_index("c")
    leaving = []
    for i, (out, (k0, k1)) in enumerate(zip((o0, o1, o2, o3), ROLES)):
        k = jnp.where(core == 0, k0, k1)
        for s in range(PAIR_MAX):
            j = k * PAIR_MAX + s

            @pl.when(live(count, k, s))
            def _():
                built[i, s] = dot(ts[tile[0, j]], dg[row[0, j]]).astype(BF)

            @pl.when(jnp.logical_not(live(count, k, s)))
            def _():
                built[i, s] = jnp.zeros(built.shape[2:], BF)

        leaving.append(pltpu.make_async_copy(built.at[i], out, sent.at[i]))
        leaving[-1].start()
    for c in (*leaving, copies[4]):
        c.wait()


def base_kernel(row, col, tile, count, own, far, dagg, tiles, turned, base, token, ds, df, ts, ws, dg, sems):
    token[...] = jnp.zeros_like(token)
    pieces = [(turned, ws), (own, ds), (far, df), (tiles, ts), (dagg, dg)]
    copies = [pltpu.make_async_copy(a, b, sems.at[i]) for i, (a, b) in enumerate(pieces)]
    for c in copies:
        c.start()
    for c in copies[:3]:
        c.wait()
    blocks = base.shape[0]
    for r in range(2):
        total = wide(ds, df, ws, r, blocks * BLOCK // 2)
        base[r * blocks // 2 : (r + 1) * blocks // 2] = total.reshape(blocks // 2, BLOCK, -1)
    for c in copies[3:]:
        c.wait()
    for s in range(PAIR_MAX):
        j = REACH * PAIR_MAX + s

        @pl.when(live(count, REACH, s))
        def _():
            base[col[0, j]] += dot(ts[tile[0, j]], dg[row[0, j]])


def place_kernel(c0, c1, c2, c3, base, r0, r1, r2, r3, out, token, acc):
    token[...] = jnp.zeros_like(token)
    core = lax.axis_index("c")
    acc[...] = base[...]
    for i, (cols, r, ks) in enumerate(zip((c0, c1, c2, c3), (r0, r1, r2, r3), ROLES)):
        sender = core if i < 2 else 1 - core
        k = jnp.where(sender == 0, ks[0], ks[1])
        for s in range(PAIR_MAX):
            acc[cols[0, k * PAIR_MAX + s]] += r[s].astype(F32)
    out[...] = acc[...].astype(BF)


def assemble_kernel(own_mine, own_swap, far_mine, far_swap, neigh, self_):
    first = lax.axis_index("c") == 0
    side = lax.axis_index("f")
    halves, planes, both, width = own_mine.shape
    piece = both // 2
    own_cols = pl.ds(pl.multiple_of(side * width, 128), width)
    far_cols = pl.ds(pl.multiple_of((1 - side) * width, 128), width)
    for out, a, b in ((neigh, own_mine, own_swap), (self_, own_swap, own_mine)):
        for p in range(planes):
            for h in range(halves):
                n = p * halves + h
                at = slice(n * piece, (n + 1) * piece)
                out[at, own_cols] = jnp.where(first, a[h, p, :piece], b[h, p, :piece]).astype(F32)
    for out, a, b in ((neigh, far_mine, far_swap), (self_, far_swap, far_mine)):
        for n in range(planes * halves):
            at = slice(n * piece, (n + 1) * piece)
            out[at, far_cols] = jnp.where(first, a[n, piece:], b[n, piece:]).astype(F32)


def run(kernel, outs, in_specs, out_specs=None, scratch=(), vmem=16, **more):
    many = isinstance(outs, list)
    return pl.pallas_call(
        kernel,
        out_shape=outs,
        in_specs=in_specs,
        out_specs=out_specs or ([VMEM] * len(outs) if many else VMEM),
        scratch_shapes=list(scratch),
        compiler_params=params(vmem),
        cost_estimate=COST,
        **more,
    )


def on_device(node_feats, edge_tiles, slot_row, slot_col, slot_tile, slot_count, w_self, w_neigh, bias, cotangent):
    nodes, width = node_feats.shape
    blocks = nodes // BLOCK
    half = width // 2
    scale = float(nodes * lax.axis_size(NODE)) ** (-0.5)
    x = node_feats.reshape(blocks, BLOCK, width)

    ints = (slot_row, slot_col, slot_tile, slot_count)
    passing = mirror(x, -REACH)
    ahead = mirror(x, REACH)
    near = swap(x, "c")
    mark = shape((8, 128), F32)
    x_t, neigh_t, self_t, tiles_t, token = run(
        turn_kernel,
        [shape((width, nodes), BF)] + [shape((2 * width, width), BF)] * 2 + [shape(edge_tiles.shape, BF), mark],
        [VMEM] * 4,
        vmem=20,
    )(node_feats, w_neigh, w_self, edge_tiles)
    acc0, part, own0, token = run(
        early_kernel,
        [shape((blocks, BLOCK, width), F32)] + [shape((nodes, width), F32)] * 2 + [mark],
        [SMEM] * 4 + [VMEM] * 5 + [ANY],
        vmem=20,
    )(*ints, x, near, edge_tiles, w_self, bias.reshape(1, width), token)

    def after(array, *others):
        return run(
            pass_kernel,
            shape(array.shape, array.dtype),
            [ANY] * (1 + len(others)),
            ANY,
            input_output_aliases={0: 0},
            vmem=2,
        )(array, *others)

    passing = after(passing, token)
    passed = swap(passing, "c")
    aggregate, send0, send1 = run(
        aggregate_kernel,
        [shape((nodes, width), BF)] + [shape((nodes, half), BF)] * 2,
        [SMEM] * 4 + [VMEM] * 7,
        scratch=[pltpu.VMEM((blocks, BLOCK, width), F32)],
        vmem=20,
    )(*ints, ahead, passing, passed, acc0, part, edge_tiles, w_neigh)
    recv = [swap(send0, "f"), swap(send1, "f")]

    tall = pl.BlockSpec((TALL, width), lambda i: (i, 0))
    own, agg_t = run(
        own_kernel,
        [shape((nodes, width), F32), shape((width, nodes), BF)],
        [tall, tall, pl.BlockSpec(w_neigh.shape, lambda i: (0, 0))],
        [tall, pl.BlockSpec((width, TALL), lambda i: (0, i))],
        grid=(nodes // TALL,),
    )(aggregate, own0, w_neigh)

    hidden, delta = None, None
    sums = []
    for c in range(2):
        column = pl.BlockSpec((TALL, half), lambda i, c=c: (i, c))
        alone = pl.BlockSpec((TALL, half), lambda i: (i, 0))
        extra = [hidden, delta] if c else []
        hidden, delta, total = run(
            act_kernel,
            [shape((nodes, width), BF), shape((nodes, width), BF), shape((8, half), F32)],
            [column, alone, column] + [ANY] * len(extra),
            [column, column, pl.BlockSpec((8, half), lambda i: (0, 0))],
            grid=(nodes // TALL,),
            input_output_aliases={3: 0, 4: 1} if c else {},
        )(own, recv[c], cotangent, *extra)
        sums.append(total)
    other = swap(delta, "f")

    plane, chips = lax.axis_size(PLANE), lax.axis_size(CHIPS)
    piece = width // plane
    strip = pl.BlockSpec((width // 2, nodes), lambda i: (i, 0))
    full = pl.BlockSpec((nodes, width), lambda i: (0, 0))
    out = pl.BlockSpec((width // 2, width), lambda i: (i, 0))
    pair = [shape((width, width), BF), shape((width, width), F32)]
    send, keep = run(weight_kernel, pair, [strip, strip, full], [out, out], grid=(2,))(agg_t, x_t, delta)
    got, *got_sums = [swap(v, "c") for v in (send, *sums)]
    steps = 4
    part = pl.BlockSpec((width // steps, width), lambda i: (i, 0))
    small = pl.BlockSpec((8, half), lambda i: (0, 0))
    parts = run(
        join_kernel,
        shape((plane, piece + 8, width), BF),
        [part, part] + [small] * 4,
        pl.BlockSpec((plane // steps, piece + 8, width), lambda i: (i, 0, 0)),
        grid=(steps,),
    )(keep, got, *sums, *got_sums)
    parts = lax.all_to_all(parts, PLANE, 0, 0)

    columns = send_roles([slot_col] * 4)
    moved = pl.BlockSpec((plane, piece + 8, width // 2), lambda i: (0, 0, i))
    summed = pl.BlockSpec((piece + 8, width // 2), lambda i: (0, i))
    send, keep, own_total, token = run(
        weight_total_kernel,
        pair + [shape((piece + 8, width), F32), mark],
        [strip, strip, full, moved] + [SMEM] * 4,
        [out, out, summed, pl.BlockSpec(mark.shape, lambda i: (0, 0))],
        grid=(2,),
        vmem=50,
    )(agg_t, x_t, other, parts, *columns)
    got = swap(send, "c")
    own_got = swap(own_total, "xl")
    *outward, dagg, token = run(
        outward_kernel,
        [shape((PAIR_MAX, BLOCK, width), BF)] * 4 + [shape((blocks, BLOCK, width), BF), mark],
        [SMEM] * 3 + [ANY] * 5,
        [ANY] * 5 + [VMEM],
        [
            pltpu.VMEM((nodes, width), BF),
            pltpu.VMEM((nodes, width), BF),
            pltpu.VMEM(edge_tiles.shape, BF),
            pltpu.VMEM(neigh_t.shape, BF),
            pltpu.VMEM((blocks, BLOCK, width), BF),
            pltpu.VMEM((4, PAIR_MAX, BLOCK, width), BF),
            pltpu.SemaphoreType.DMA((5,)),
            pltpu.SemaphoreType.DMA((4,)),
        ],
        vmem=56,
    )(slot_row, slot_tile, slot_count, delta, other, tiles_t, neigh_t, token)
    returned = send_roles(outward)
    parts = run(
        join_kernel,
        shape((chips, width // chips, width), BF),
        [part, part, ANY],
        pl.BlockSpec((chips // steps, width // chips, width), lambda i: (i, 0, 0)),
        grid=(steps,),
    )(keep, got, token)
    far_parts = lax.all_to_all(parts, CHIPS, 0, 0)

    base, token = run(
        base_kernel,
        [shape((blocks, BLOCK, width), F32), mark],
        [SMEM] * 4 + [ANY] * 5,
        [VMEM, VMEM],
        [
            pltpu.VMEM((nodes, width), BF),
            pltpu.VMEM((nodes, width), BF),
            pltpu.VMEM(edge_tiles.shape, BF),
            pltpu.VMEM(self_t.shape, BF),
            pltpu.VMEM((blocks, BLOCK, width), BF),
            pltpu.SemaphoreType.DMA((5,)),
        ],
        vmem=56,
    )(*ints, delta, other, dagg, tiles_t, self_t)

    corner = pl.BlockSpec((1, 16, BLOCK), lambda i: (0, 0, 0))
    arrived = run(
        mark_kernel, mark, [corner] * 4, pl.BlockSpec(mark.shape, lambda i: (0, 0)), grid=(1,), vmem=4
    )(*returned)
    spread, grad_bias = run(
        lambda *refs: spread_kernel(scale, *refs),
        [shape((chips, piece, width), BF), shape((1, width), F32)],
        [summed, summed, pl.BlockSpec((chips, width // chips, width // 2), lambda i: (0, 0, i)), ANY, ANY],
        [
            pl.BlockSpec((chips, piece, width // 2), lambda i: (0, 0, i)),
            pl.BlockSpec((1, width // 2), lambda i: (0, i)),
        ],
        grid=(2,),
    )(own_total, own_got, far_parts, token, arrived)
    column = pl.BlockSpec((blocks, BLOCK, BLOCK), lambda i: (0, 0, i))
    narrow = pl.BlockSpec((PAIR_MAX, BLOCK, BLOCK), lambda i: (0, 0, i))
    grad_nodes, token = run(
        place_kernel,
        [shape((blocks, BLOCK, width), BF), mark],
        [SMEM] * 4 + [column] + [narrow] * 4,
        [column, pl.BlockSpec(mark.shape, lambda i: (0, 0))],
        [pltpu.VMEM((blocks, BLOCK, BLOCK), F32)],
        grid=(width // BLOCK,),
    )(*columns, base, *returned)
    grad_nodes = grad_nodes.reshape(nodes, width)

    mine = after(lax.all_to_all(spread, CHIPS, 0, 0), token)
    swapped = swap(mine, "c")

    halves = lax.axis_size("xl")
    block = pl.BlockSpec((halves, plane // steps, piece, width), lambda i: (0, i, 0, 0))
    rows = pl.BlockSpec((width // steps, 2 * width), lambda i: (i, 0))
    by_chip = pl.BlockSpec((chips // steps, piece, width), lambda i: (i, 0, 0))
    view = (halves, plane, piece, width)
    grads = run(
        assemble_kernel,
        [shape((width, 2 * width), F32)] * 2,
        [block, block, by_chip, by_chip],
        [rows, rows],
        grid=(steps,),
    )(mine.reshape(view), swapped.reshape(view), mine, swapped)
    grad_neigh, grad_self = grads
    return hidden, grad_nodes, grad_self, grad_neigh, grad_bias.reshape(width)


def solution(mesh):
    fine = Mesh(mesh.devices.reshape(2, 4, 4, 2, 2), (*NODE, "f"))
    placed = (
        P(NODE, "f"),
        P(NODE, None, None),
        P(NODE, None),
        P(NODE, None),
        P(NODE, None),
        P(NODE, None),
        P("f", None),
        P("f", None),
        P("f"),
        P(NODE, "f"),
    )
    return jax.shard_map(
        on_device,
        mesh=fine,
        in_specs=placed,
        out_specs=(P(NODE, "f"), P(NODE, "f"), P("f", None), P("f", None), P("f")),
        check_vma=False,
    )
```

```python
import jax
import jax.numpy as jnp
from jax import lax
from jax.experimental import pallas as pl
from jax.experimental.pallas import tpu as pltpu
from jax.sharding import Mesh, PartitionSpec as P

REACH = 2
PAIR_MAX = 4
BLOCK = 128
NODE = ("xl", "z", "y", "c")
CHIPS = ("xl", "z", "y")
PLANE = ("z", "y")
VMEM = pl.BlockSpec(memory_space=pltpu.VMEM)
SMEM = pl.BlockSpec(memory_space=pltpu.SMEM)
HBM = pl.BlockSpec(memory_space=pltpu.HBM)
ANY = pl.BlockSpec(memory_space=pl.ANY)
BF = jnp.bfloat16
F32 = jnp.float32
MIB = 1 << 20
ROLES = ((4, 0), (0, 4), (1, 3), (3, 1))
TALL = 256
LONG = 20000000000


def dot(a, b, dims=((1,), (0,))):
    return lax.dot_general(a, b, (dims, ((), ())), preferred_element_type=F32)


def mirror(block, distance):
    count = lax.axis_size(NODE)
    return lax.ppermute(
        block, NODE, [(i, (i + (distance if i % 2 == 0 else -distance)) % count) for i in range(count)]
    )


def swap(block, axis):
    return lax.ppermute(block, axis, [(0, 1), (1, 0)])


def send_roles(blocks):
    ahead, behind, outer, sibling = blocks
    return [mirror(ahead, REACH), mirror(behind, -REACH), mirror(outer, -1), swap(sibling, "c")]


def shape(dims, kind):
    return jax.ShapeDtypeStruct(dims, kind)


def params(vmem):
    return pltpu.CompilerParams(vmem_limit_bytes=vmem * MIB)


def live(count, k, s):
    return s < count[0, k]


def pass_kernel(array, *rest):
    pass


def turn_kernel(x, w_neigh, w_self, tiles, x_t, neigh_t, self_t, tiles_t, token):
    x_t[...] = x[...].T
    neigh_t[...] = w_neigh[...].T
    self_t[...] = w_self[...].T
    for j in range(tiles.shape[0]):
        tiles_t[j] = tiles[j].T
    token[...] = jnp.zeros_like(token)


def early_kernel(row, col, tile, count, x, near, tiles, w_self, bias, after, acc, ahead, own, token):
    token[...] = jnp.zeros_like(token)
    core = lax.axis_index("c")
    acc[...] = jnp.zeros_like(acc)
    for k, source in ((REACH, x), (jnp.where(core == 0, 3, 1), near)):
        for s in range(PAIR_MAX):
            j = k * PAIR_MAX + s

            @pl.when(live(count, k, s))
            def _():
                acc[row[0, j]] += dot(tiles[tile[0, j]], source[col[0, j]])

    width = own.shape[1]
    side = lax.axis_index("f")
    rows = TALL
    for r in range(own.shape[0] // rows):
        at = slice(r * rows, (r + 1) * rows)
        mine = x[r * rows // BLOCK : (r + 1) * rows // BLOCK].reshape(rows, width)
        ahead[at, :] = dot(mine, w_self[:, pl.ds(pl.multiple_of((1 - side) * width, 128), width)])
        own[at, :] = dot(mine, w_self[:, pl.ds(pl.multiple_of(side * width, 128), width)]) + bias[...]


def aggregate_kernel(row, col, tile, count, ahead, passing, passed, acc0, part, tiles, w_neigh, agg, send0, send1, acc):
    core = lax.axis_index("c")
    acc[...] = acc0[...]
    for (k0, k1), source in zip(((0, 4), (4, 0), (1, 3)), (ahead, passing, passed)):
        k = jnp.where(core == 0, k0, k1)
        for s in range(PAIR_MAX):
            j = k * PAIR_MAX + s

            @pl.when(live(count, k, s))
            def _():
                acc[row[0, j]] += dot(tiles[tile[0, j]], source[col[0, j]])

    rows = acc.shape[0] * BLOCK // 2
    half = send0.shape[1]
    agg[...] = acc[...].astype(BF).reshape(agg.shape)
    other = (1 - lax.axis_index("f")) * (2 * half)
    for c, send in enumerate((send0, send1)):
        cols = pl.ds(pl.multiple_of(other + c * half, 128), half)
        span = slice(c * half, (c + 1) * half)
        for r in range(2):
            at = slice(r * rows, (r + 1) * rows)
            send[at, :] = (dot(agg[at, :], w_neigh[:, cols]) + part[at, span]).astype(BF)


def own_kernel(agg, own0, w_neigh, out, agg_t):
    width = out.shape[1]
    cols = pl.ds(pl.multiple_of(lax.axis_index("f") * width, 128), width)
    out[...] = dot(agg[...], w_neigh[:, cols]) + own0[...]
    agg_t[...] = agg[...].T


def act_kernel(own, recv, cot, *rest):
    hidden, delta, sums = rest[-3:]
    pre = own[...] + recv[...].astype(F32)
    sigma = jax.nn.sigmoid(pre)
    hidden[...] = (pre * sigma).astype(BF)
    d = (cot[...].astype(F32) * sigma * (1.0 + pre * (1.0 - sigma))).astype(BF)
    delta[...] = d

    @pl.when(pl.program_id(0) == 0)
    def _():
        sums[...] = jnp.zeros_like(sums)

    sums[...] += jnp.sum(d.astype(F32).reshape(-1, 8, d.shape[1]), axis=0)


def weight_kernel(agg_t, x_t, d, *rest):
    send, keep = rest[-2:]
    first = lax.axis_index("c") == 0
    neigh = dot(agg_t[...], d[...])
    own = dot(x_t[...], d[...])
    send[...] = jnp.where(first, own, neigh).astype(BF)
    keep[...] = jnp.where(first, neigh, own)


def weight_total_kernel(agg_t, x_t, d, moved, send, keep, total):
    weight_kernel(agg_t, x_t, d, send, keep)
    total[...] = jnp.sum(moved[...].astype(F32), axis=0)


def bias_rows(sums):
    total = jnp.sum(sums, axis=0, keepdims=True)
    high = total.astype(BF)
    low = (total - high.astype(F32)).astype(BF)
    row = lax.broadcasted_iota(jnp.int32, (8, total.shape[1]), 0)
    return jnp.where(row == 0, high.astype(F32), jnp.where(row == 1, low.astype(F32), 0.0)).astype(BF)


def join_kernel(keep, got, *rest):
    out = rest[-1]
    pieces, tall, width = out.shape
    piece = keep.shape[0] // pieces
    both = (keep[...] + got[...].astype(F32)).astype(BF)
    out[:, :piece, :] = both.reshape(pieces, piece, width)
    if tall > piece:
        s0, s1, g0, g1 = rest[:-1]
        half = s0.shape[1]
        for c, (s, g) in enumerate(((s0, g0), (s1, g1))):
            rows = bias_rows(jnp.concatenate([s[...], g[...]], axis=0))
            out[:, piece:, c * half : (c + 1) * half] = jnp.broadcast_to(rows[None], (pieces, 8, half))


def spread_kernel(scale, a, b, moved, after, out, bias):
    piece = out.shape[1] // 2
    xl = lax.axis_index("xl")
    rows = pl.ds(pl.multiple_of(xl * piece, piece), piece)
    mine = (a[rows, :] + b[rows, :]) * scale
    far = jnp.sum(moved[...].astype(F32), axis=0) * scale
    out[:, :piece, :] = jnp.broadcast_to(mine.astype(BF)[None], (out.shape[0], *mine.shape))
    out[:, piece:, :] = jnp.broadcast_to(far.astype(BF)[None], (out.shape[0], *far.shape))
    bias[...] = jnp.sum((a[2 * piece :, :] + b[2 * piece :, :]) * scale, axis=0, keepdims=True)


def wide(own, far, turned, r, rows):
    side = lax.axis_index("f")
    width = own.shape[1]
    at = slice(r * rows, (r + 1) * rows)
    mine = turned[pl.ds(pl.multiple_of(side * width, 128), width), :]
    other = turned[pl.ds(pl.multiple_of((1 - side) * width, 128), width), :]
    return dot(own[at, :], mine) + dot(far[at, :], other)


def outward_kernel(
    row, col, tile, count, own, far, tiles, turned, after,
    o0, o1, o2, o3, dagg, token, ds, df, ts, wn, dg, total, built, sems, sent,
):
    token[...] = jnp.zeros_like(token)
    width = own.shape[1]
    rows = own.shape[0] // 2
    side = lax.axis_index("f")
    copies = []
    for n, (d, held, start) in enumerate(((own, ds, side), (far, df, 1 - side))):
        span = pl.ds(pl.multiple_of(start * width, 128), width)
        copies.append(pltpu.make_async_copy(turned.at[span, :], wn.at[n], sems.at[3 * n]))
        for r in range(2):
            at = pl.ds(r * rows, rows)
            copies.append(pltpu.make_async_copy(d.at[at, :], held.at[at, :], sems.at[3 * n + 1 + r]))
    copies.append(pltpu.make_async_copy(tiles, ts, sems.at[6]))
    copies.append(pltpu.make_async_copy(dg, dagg, sems.at[7]))
    for c in copies[:7]:
        c.start()
    copies[0].wait()
    for r in range(2):
        copies[1 + r].wait()
        at = slice(r * rows, (r + 1) * rows)
        total[at, :] = dot(ds[at, :], wn[0])
    copies[3].wait()
    blocks = dg.shape[0] // 2
    for r in range(2):
        copies[4 + r].wait()
        at = slice(r * rows, (r + 1) * rows)
        both = total[at, :] + dot(df[at, :], wn[1])
        dg[r * blocks : (r + 1) * blocks] = both.astype(BF).reshape(blocks, BLOCK, width)
    copies[7].start()
    copies[6].wait()
    core = lax.axis_index("c")
    leaving = []
    line = lax.broadcasted_iota(jnp.int32, (built.shape[1] - PAIR_MAX * BLOCK, width), 0)
    for i, (out, (k0, k1)) in enumerate(zip((o0, o1, o2, o3), ROLES)):
        k = jnp.where(core == 0, k0, k1)
        places = jnp.zeros(line.shape, F32)
        for s in range(PAIR_MAX):
            j = k * PAIR_MAX + s
            at = slice(s * BLOCK, (s + 1) * BLOCK)

            @pl.when(live(count, k, s))
            def _():
                built[i, at] = dot(ts[tile[0, j]], dg[row[0, j]]).astype(BF)

            @pl.when(jnp.logical_not(live(count, k, s)))
            def _():
                built[i, at] = jnp.zeros((BLOCK, width), BF)

            places = jnp.where(line == s, col[0, j].astype(F32), places)
        built[i, PAIR_MAX * BLOCK :] = places.astype(BF)
        leaving.append(pltpu.make_async_copy(built.at[i], out, sent.at[i]))
        leaving[-1].start()
    for c in (*leaving, copies[7]):
        c.wait()


def base_kernel(row, col, tile, count, own, far, dagg, tiles, turned, base, ds, df, ts, ws, dg, sems):
    pieces = [(turned, ws), (own, ds), (far, df), (tiles, ts), (dagg, dg)]
    copies = [pltpu.make_async_copy(a, b, sems.at[i]) for i, (a, b) in enumerate(pieces)]
    for c in copies:
        c.start()
    for c in copies[:3]:
        c.wait()
    blocks = base.shape[0]
    for r in range(2):
        total = wide(ds, df, ws, r, blocks * BLOCK // 2)
        base[r * blocks // 2 : (r + 1) * blocks // 2] = total.reshape(blocks // 2, BLOCK, -1)
    for c in copies[3:]:
        c.wait()
    for s in range(PAIR_MAX):
        j = REACH * PAIR_MAX + s

        @pl.when(live(count, REACH, s))
        def _():
            base[col[0, j]] += dot(ts[tile[0, j]], dg[row[0, j]])


def place_kernel(base, r0, r1, r2, r3, out, token, acc, places):
    token[...] = jnp.zeros_like(token)

    @pl.when(pl.program_id(0) == 0)
    def _():
        for i, r in enumerate((r0, r1, r2, r3)):
            for s in range(PAIR_MAX):
                line = PAIR_MAX * BLOCK + s
                places[i, s] = jnp.max(r[line : line + 1, :].astype(F32)).astype(jnp.int32)

    acc[...] = base[...]
    for i, r in enumerate((r0, r1, r2, r3)):
        for s in range(PAIR_MAX):
            acc[places[i, s]] += r[s * BLOCK : (s + 1) * BLOCK, :].astype(F32)
    out[...] = acc[...].astype(BF)


def assemble_kernel(own_mine, own_swap, far_mine, far_swap, neigh, self_):
    first = lax.axis_index("c") == 0
    side = lax.axis_index("f")
    halves, planes, both, width = own_mine.shape
    piece = both // 2
    own_cols = pl.ds(pl.multiple_of(side * width, 128), width)
    far_cols = pl.ds(pl.multiple_of((1 - side) * width, 128), width)
    for out, a, b in ((neigh, own_mine, own_swap), (self_, own_swap, own_mine)):
        for p in range(planes):
            for h in range(halves):
                n = p * halves + h
                at = slice(n * piece, (n + 1) * piece)
                out[at, own_cols] = jnp.where(first, a[h, p, :piece], b[h, p, :piece]).astype(F32)
    for out, a, b in ((neigh, far_mine, far_swap), (self_, far_swap, far_mine)):
        for n in range(planes * halves):
            at = slice(n * piece, (n + 1) * piece)
            out[at, far_cols] = jnp.where(first, a[n, piece:], b[n, piece:]).astype(F32)


def run(kernel, outs, in_specs, out_specs=None, scratch=(), vmem=16, flops=10**4, **more):
    many = isinstance(outs, list)
    return pl.pallas_call(
        kernel,
        out_shape=outs,
        in_specs=in_specs,
        out_specs=out_specs or ([VMEM] * len(outs) if many else VMEM),
        scratch_shapes=list(scratch),
        compiler_params=params(vmem),
        cost_estimate=pl.CostEstimate(flops=flops, bytes_accessed=10**4, transcendentals=0),
        **more,
    )


def on_device(node_feats, edge_tiles, slot_row, slot_col, slot_tile, slot_count, w_self, w_neigh, bias, cotangent):
    nodes, width = node_feats.shape
    blocks = nodes // BLOCK
    half = width // 2
    scale = float(nodes * lax.axis_size(NODE)) ** (-0.5)
    x = node_feats.reshape(blocks, BLOCK, width)

    ints = (slot_row, slot_col, slot_tile, slot_count)
    passing = mirror(x, -REACH)
    ahead = mirror(x, REACH)
    near = swap(x, "c")
    mark = shape((8, 128), F32)
    x_t, neigh_t, self_t, tiles_t, token = run(
        turn_kernel,
        [shape((width, nodes), BF)] + [shape((2 * width, width), BF)] * 2 + [shape(edge_tiles.shape, BF), mark],
        [VMEM] * 4,
        vmem=20,
    )(node_feats, w_neigh, w_self, edge_tiles)
    acc0, part, own0, token = run(
        early_kernel,
        [shape((blocks, BLOCK, width), F32)] + [shape((nodes, width), F32)] * 2 + [mark],
        [SMEM] * 4 + [VMEM] * 5 + [ANY],
        vmem=20,
    )(*ints, x, near, edge_tiles, w_self, bias.reshape(1, width), token)

    def after(array, *others, flops=10**4):
        return run(
            pass_kernel,
            shape(array.shape, array.dtype),
            [ANY] * (1 + len(others)),
            ANY,
            input_output_aliases={0: 0},
            vmem=2,
            flops=flops,
        )(array, *others)

    passing = after(passing, token, ahead)
    passed = swap(passing, "c")
    aggregate, send0, send1 = run(
        aggregate_kernel,
        [shape((nodes, width), BF)] + [shape((nodes, half), BF)] * 2,
        [SMEM] * 4 + [VMEM] * 7,
        scratch=[pltpu.VMEM((blocks, BLOCK, width), F32)],
        vmem=20,
    )(*ints, ahead, passing, passed, acc0, part, edge_tiles, w_neigh)
    recv = [swap(send0, "f"), swap(send1, "f")]

    tall = pl.BlockSpec((TALL, width), lambda i: (i, 0))
    own, agg_t = run(
        own_kernel,
        [shape((nodes, width), F32), shape((width, nodes), BF)],
        [tall, tall, pl.BlockSpec(w_neigh.shape, lambda i: (0, 0))],
        [tall, pl.BlockSpec((width, TALL), lambda i: (0, i))],
        grid=(nodes // TALL,),
    )(aggregate, own0, w_neigh)

    hidden, delta = None, None
    sums = []
    for c in range(2):
        column = pl.BlockSpec((TALL, half), lambda i, c=c: (i, c))
        alone = pl.BlockSpec((TALL, half), lambda i: (i, 0))
        extra = [hidden, delta] if c else []
        hidden, delta, total = run(
            act_kernel,
            [shape((nodes, width), BF), shape((nodes, width), BF), shape((8, half), F32)],
            [column, alone, column] + [ANY] * len(extra),
            [column, column, pl.BlockSpec((8, half), lambda i: (0, 0))],
            grid=(nodes // TALL,),
            input_output_aliases={3: 0, 4: 1} if c else {},
        )(own, recv[c], cotangent, *extra)
        sums.append(total)
    other = after(swap(delta, "f"), flops=LONG)

    plane, chips = lax.axis_size(PLANE), lax.axis_size(CHIPS)
    piece = width // plane
    strip = pl.BlockSpec((width // 2, nodes), lambda i: (i, 0))
    full = pl.BlockSpec((nodes, width), lambda i: (0, 0))
    out = pl.BlockSpec((width // 2, width), lambda i: (i, 0))
    pair = [shape((width, width), BF), shape((width, width), F32)]
    send, keep = run(weight_kernel, pair, [strip, strip, full], [out, out], grid=(2,))(agg_t, x_t, delta)
    got, *got_sums = [swap(v, "c") for v in (send, *sums)]
    steps = 4
    part = pl.BlockSpec((width // steps, width), lambda i: (i, 0))
    small = pl.BlockSpec((8, half), lambda i: (0, 0))
    parts = run(
        join_kernel,
        shape((plane, piece + 8, width), BF),
        [part, part] + [small] * 4,
        pl.BlockSpec((plane // steps, piece + 8, width), lambda i: (i, 0, 0)),
        grid=(steps,),
    )(keep, got, *sums, *got_sums)
    parts = lax.all_to_all(parts, PLANE, 0, 0)

    moved = pl.BlockSpec((plane, piece + 8, width // 2), lambda i: (0, 0, i))
    summed = pl.BlockSpec((piece + 8, width // 2), lambda i: (0, i))
    send, keep, own_total = run(
        weight_total_kernel,
        pair + [shape((piece + 8, width), F32)],
        [strip, strip, full, moved],
        [out, out, summed],
        grid=(2,),
        vmem=50,
    )(agg_t, x_t, other, parts)
    got = swap(send, "c")
    own_got = after(swap(own_total, "xl"), flops=2*10**10)
    parts = run(
        join_kernel,
        shape((chips, width // chips, width), BF),
        [part, part],
        pl.BlockSpec((chips // steps, width // chips, width), lambda i: (i, 0, 0)),
        grid=(steps,),
    )(keep, got)
    far_parts = lax.all_to_all(parts, CHIPS, 0, 0)

    tall_term = PAIR_MAX * BLOCK + 16
    *outward, dagg, token = run(
        outward_kernel,
        [shape((tall_term, width), BF)] * 4 + [shape((blocks, BLOCK, width), BF), mark],
        [SMEM] * 4 + [ANY] * 5,
        [ANY] * 5 + [VMEM],
        [
            pltpu.VMEM((nodes, width), BF),
            pltpu.VMEM((nodes, width), BF),
            pltpu.VMEM(edge_tiles.shape, BF),
            pltpu.VMEM((2, width, width), BF),
            pltpu.VMEM((blocks, BLOCK, width), BF),
            pltpu.VMEM((nodes, width), F32),
            pltpu.VMEM((4, tall_term, width), BF),
            pltpu.SemaphoreType.DMA((8,)),
            pltpu.SemaphoreType.DMA((4,)),
        ],
        vmem=56,
    )(*ints, delta, other, tiles_t, neigh_t, parts)
    returned = send_roles(outward)

    base = run(
        base_kernel,
        shape((blocks, BLOCK, width), F32),
        [SMEM] * 4 + [ANY] * 5,
        VMEM,
        [
            pltpu.VMEM((nodes, width), BF),
            pltpu.VMEM((nodes, width), BF),
            pltpu.VMEM(edge_tiles.shape, BF),
            pltpu.VMEM(self_t.shape, BF),
            pltpu.VMEM((blocks, BLOCK, width), BF),
            pltpu.SemaphoreType.DMA((5,)),
        ],
        vmem=56,
    )(*ints, delta, other, dagg, tiles_t, self_t)

    spread, grad_bias = run(
        lambda *refs: spread_kernel(scale, *refs),
        [shape((chips, piece, width), BF), shape((1, width), F32)],
        [summed, summed, pl.BlockSpec((chips, width // chips, width // 2), lambda i: (0, 0, i)), ANY],
        [
            pl.BlockSpec((chips, piece, width // 2), lambda i: (0, 0, i)),
            pl.BlockSpec((1, width // 2), lambda i: (0, i)),
        ],
        grid=(2,),
    )(own_total, own_got, far_parts, token)
    column = pl.BlockSpec((blocks, BLOCK, BLOCK), lambda i: (0, 0, i))
    narrow = pl.BlockSpec((tall_term, BLOCK), lambda i: (0, i))
    grad_nodes, token = run(
        place_kernel,
        [shape((blocks, BLOCK, width), BF), mark],
        [column] + [narrow] * 4,
        [column, pl.BlockSpec(mark.shape, lambda i: (0, 0))],
        [pltpu.VMEM((blocks, BLOCK, BLOCK), F32), pltpu.SMEM((4, PAIR_MAX), jnp.int32)],
        grid=(width // BLOCK,),
        vmem=56,
        flops=9*10**9,
    )(base, *returned)
    grad_nodes = grad_nodes.reshape(nodes, width)

    mine = after(lax.all_to_all(spread, CHIPS, 0, 0), token)
    swapped = swap(mine, "c")

    halves = lax.axis_size("xl")
    block = pl.BlockSpec((halves, plane // steps, piece, width), lambda i: (0, i, 0, 0))
    rows = pl.BlockSpec((width // steps, 2 * width), lambda i: (i, 0))
    by_chip = pl.BlockSpec((chips // steps, piece, width), lambda i: (i, 0, 0))
    view = (halves, plane, piece, width)
    grads = run(
        assemble_kernel,
        [shape((width, 2 * width), F32)] * 2,
        [block, block, by_chip, by_chip],
        [rows, rows],
        grid=(steps,),
    )(mine.reshape(view), swapped.reshape(view), mine, swapped)
    grad_neigh, grad_self = grads
    return hidden, grad_nodes, grad_self, grad_neigh, grad_bias.reshape(width)


def solution(mesh):
    fine = Mesh(mesh.devices.reshape(2, 4, 4, 2, 2), (*NODE, "f"))
    placed = (
        P(NODE, "f"),
        P(NODE, None, None),
        P(NODE, None),
        P(NODE, None),
        P(NODE, None),
        P(NODE, None),
        P("f", None),
        P("f", None),
        P("f"),
        P(NODE, "f"),
    )
    return jax.shard_map(
        on_device,
        mesh=fine,
        in_specs=placed,
        out_specs=(P(NODE, "f"), P(NODE, "f"), P("f", None), P("f", None), P("f")),
        check_vma=False,
    )
```

```python
import jax
import jax.numpy as jnp
from jax import lax
from jax.experimental import pallas as pl
from jax.experimental.pallas import tpu as pltpu
from jax.sharding import Mesh, PartitionSpec as P

REACH = 2
PAIR_MAX = 4
BLOCK = 128
NODE = ("xl", "z", "y", "c")
CHIPS = ("xl", "z", "y")
PLANE = ("z", "y")
VMEM = pl.BlockSpec(memory_space=pltpu.VMEM)
SMEM = pl.BlockSpec(memory_space=pltpu.SMEM)
HBM = pl.BlockSpec(memory_space=pltpu.HBM)
ANY = pl.BlockSpec(memory_space=pl.ANY)
BF = jnp.bfloat16
F32 = jnp.float32
MIB = 1 << 20
ROLES = ((4, 0), (0, 4), (1, 3), (3, 1))
TALL = 256
LONG = 20000000000


def dot(a, b, dims=((1,), (0,))):
    return lax.dot_general(a, b, (dims, ((), ())), preferred_element_type=F32)


def mirror(block, distance):
    count = lax.axis_size(NODE)
    return lax.ppermute(
        block, NODE, [(i, (i + (distance if i % 2 == 0 else -distance)) % count) for i in range(count)]
    )


def swap(block, axis):
    return lax.ppermute(block, axis, [(0, 1), (1, 0)])


def send_roles(blocks):
    ahead, behind, outer, sibling = blocks
    return [mirror(ahead, REACH), mirror(behind, -REACH), mirror(outer, -1), swap(sibling, "c")]


def shape(dims, kind):
    return jax.ShapeDtypeStruct(dims, kind)


def params(vmem):
    return pltpu.CompilerParams(vmem_limit_bytes=vmem * MIB)


def live(count, k, s):
    return s < count[0, k]


def pass_kernel(array, *rest):
    pass


def turn_kernel(wanted, x, w_neigh, w_self, tiles, x_t, neigh_t, self_t, tiles_t, token):
    x_t[...] = x[...].T
    neigh_t[...] = w_neigh[...].T
    self_t[...] = w_self[...].T
    for j in range(tiles.shape[0]):
        tiles_t[j] = tiles[j].T
    token[...] = jnp.zeros_like(token)


def early_kernel(row, col, tile, count, x, near, tiles, w_self, bias, after, acc, ahead, own, token):
    token[...] = jnp.zeros_like(token)
    core = lax.axis_index("c")
    acc[...] = jnp.zeros_like(acc)
    for k, source in ((REACH, x), (jnp.where(core == 0, 3, 1), near)):
        for s in range(PAIR_MAX):
            j = k * PAIR_MAX + s

            @pl.when(live(count, k, s))
            def _():
                acc[row[0, j]] += dot(tiles[tile[0, j]], source[col[0, j]])

    width = own.shape[1]
    side = lax.axis_index("f")
    rows = TALL
    for r in range(own.shape[0] // rows):
        at = slice(r * rows, (r + 1) * rows)
        mine = x[r * rows // BLOCK : (r + 1) * rows // BLOCK].reshape(rows, width)
        ahead[at, :] = dot(mine, w_self[:, pl.ds(pl.multiple_of((1 - side) * width, 128), width)])
        own[at, :] = dot(mine, w_self[:, pl.ds(pl.multiple_of(side * width, 128), width)]) + bias[...]


def pick_kernel(wanted, x, after, out):
    k = jnp.where(lax.axis_index("c") == 0, 0, 4)
    for s in range(PAIR_MAX):
        out[s] = x[wanted[0, k * PAIR_MAX + s]]


def aggregate_kernel(row, col, tile, count, outer, passed, chosen, acc0, part, tiles, w_neigh, agg, send0, send1, acc):
    core = lax.axis_index("c")
    acc[...] = acc0[...]
    for (k0, k1), source in zip(((0, 4), (1, 3), (4, 0)), (chosen, outer, passed)):
        k = jnp.where(core == 0, k0, k1)
        for s in range(PAIR_MAX):
            j = k * PAIR_MAX + s

            @pl.when(live(count, k, s))
            def _():
                block = source[s] if source is chosen else source[col[0, j]]
                acc[row[0, j]] += dot(tiles[tile[0, j]], block)

    rows = acc.shape[0] * BLOCK // 2
    half = send0.shape[1]
    agg[...] = acc[...].astype(BF).reshape(agg.shape)
    other = (1 - lax.axis_index("f")) * (2 * half)
    for c, send in enumerate((send0, send1)):
        cols = pl.ds(pl.multiple_of(other + c * half, 128), half)
        span = slice(c * half, (c + 1) * half)
        for r in range(2):
            at = slice(r * rows, (r + 1) * rows)
            send[at, :] = (dot(agg[at, :], w_neigh[:, cols]) + part[at, span]).astype(BF)


def own_kernel(agg, own0, w_neigh, out, agg_t):
    width = out.shape[1]
    cols = pl.ds(pl.multiple_of(lax.axis_index("f") * width, 128), width)
    out[...] = dot(agg[...], w_neigh[:, cols]) + own0[...]
    agg_t[...] = agg[...].T


def act_kernel(own, recv, cot, *rest):
    hidden, delta, sums = rest[-3:]
    pre = own[...] + recv[...].astype(F32)
    sigma = jax.nn.sigmoid(pre)
    hidden[...] = (pre * sigma).astype(BF)
    d = (cot[...].astype(F32) * sigma * (1.0 + pre * (1.0 - sigma))).astype(BF)
    delta[...] = d

    @pl.when(pl.program_id(0) == 0)
    def _():
        sums[...] = jnp.zeros_like(sums)

    sums[...] += jnp.sum(d.astype(F32).reshape(-1, 8, d.shape[1]), axis=0)


def weight_kernel(agg_t, x_t, d, *rest):
    send, keep = rest[-2:]
    first = lax.axis_index("c") == 0
    neigh = dot(agg_t[...], d[...])
    own = dot(x_t[...], d[...])
    send[...] = jnp.where(first, own, neigh).astype(BF)
    keep[...] = jnp.where(first, neigh, own)


def weight_total_kernel(agg_t, x_t, d, moved, send, keep, total):
    weight_kernel(agg_t, x_t, d, send, keep)
    total[...] = jnp.sum(moved[...].astype(F32), axis=0)


def bias_rows(sums):
    total = jnp.sum(sums, axis=0, keepdims=True)
    high = total.astype(BF)
    low = (total - high.astype(F32)).astype(BF)
    row = lax.broadcasted_iota(jnp.int32, (8, total.shape[1]), 0)
    return jnp.where(row == 0, high.astype(F32), jnp.where(row == 1, low.astype(F32), 0.0)).astype(BF)


def join_kernel(keep, got, *rest):
    out = rest[-1]
    pieces, tall, width = out.shape
    piece = keep.shape[0] // pieces
    both = (keep[...] + got[...].astype(F32)).astype(BF)
    out[:, :piece, :] = both.reshape(pieces, piece, width)
    if tall > piece:
        s0, s1, g0, g1 = rest[:-1]
        half = s0.shape[1]
        for c, (s, g) in enumerate(((s0, g0), (s1, g1))):
            rows = bias_rows(jnp.concatenate([s[...], g[...]], axis=0))
            out[:, piece:, c * half : (c + 1) * half] = jnp.broadcast_to(rows[None], (pieces, 8, half))


def spread_kernel(scale, a, b, moved, out, bias):
    piece = out.shape[1] // 2
    xl = lax.axis_index("xl")
    rows = pl.ds(pl.multiple_of(xl * piece, piece), piece)
    mine = (a[rows, :] + b[rows, :]) * scale
    far = jnp.sum(moved[...].astype(F32), axis=0) * scale
    out[:, :piece, :] = jnp.broadcast_to(mine.astype(BF)[None], (out.shape[0], *mine.shape))
    out[:, piece:, :] = jnp.broadcast_to(far.astype(BF)[None], (out.shape[0], *far.shape))
    bias[...] = jnp.sum((a[2 * piece :, :] + b[2 * piece :, :]) * scale, axis=0, keepdims=True)


def wide(own, far, turned, r, rows):
    side = lax.axis_index("f")
    width = own.shape[1]
    at = slice(r * rows, (r + 1) * rows)
    mine = turned[pl.ds(pl.multiple_of(side * width, 128), width), :]
    other = turned[pl.ds(pl.multiple_of((1 - side) * width, 128), width), :]
    return dot(own[at, :], mine) + dot(far[at, :], other)


def outward_kernel(
    row, col, tile, count, own, far, tiles, turned, after,
    o0, o1, o2, o3, dagg, ds, df, ts, wn, dg, total, built, sems, sent,
):
    width = own.shape[1]
    rows = own.shape[0] // 2
    side = lax.axis_index("f")
    copies = []
    for n, (d, held, start) in enumerate(((own, ds, side), (far, df, 1 - side))):
        span = pl.ds(pl.multiple_of(start * width, 128), width)
        copies.append(pltpu.make_async_copy(turned.at[span, :], wn.at[n], sems.at[3 * n]))
        for r in range(2):
            at = pl.ds(r * rows, rows)
            copies.append(pltpu.make_async_copy(d.at[at, :], held.at[at, :], sems.at[3 * n + 1 + r]))
    copies.append(pltpu.make_async_copy(tiles, ts, sems.at[6]))
    copies.append(pltpu.make_async_copy(dg, dagg, sems.at[7]))
    for c in copies[:7]:
        c.start()
    copies[0].wait()
    for r in range(2):
        copies[1 + r].wait()
        at = slice(r * rows, (r + 1) * rows)
        total[at, :] = dot(ds[at, :], wn[0])
    copies[3].wait()
    blocks = dg.shape[0] // 2
    for r in range(2):
        copies[4 + r].wait()
        at = slice(r * rows, (r + 1) * rows)
        both = total[at, :] + dot(df[at, :], wn[1])
        dg[r * blocks : (r + 1) * blocks] = both.astype(BF).reshape(blocks, BLOCK, width)
    copies[7].start()
    copies[6].wait()
    core = lax.axis_index("c")
    leaving = []
    line = lax.broadcasted_iota(jnp.int32, (built.shape[1] - PAIR_MAX * BLOCK, width), 0)
    for i, (out, (k0, k1)) in enumerate(zip((o0, o1, o2, o3), ROLES)):
        k = jnp.where(core == 0, k0, k1)
        places = jnp.zeros(line.shape, F32)
        for s in range(PAIR_MAX):
            j = k * PAIR_MAX + s
            at = slice(s * BLOCK, (s + 1) * BLOCK)

            @pl.when(live(count, k, s))
            def _():
                built[i, at] = dot(ts[tile[0, j]], dg[row[0, j]]).astype(BF)

            @pl.when(jnp.logical_not(live(count, k, s)))
            def _():
                built[i, at] = jnp.zeros((BLOCK, width), BF)

            places = jnp.where(line == s, col[0, j].astype(F32), places)
        built[i, PAIR_MAX * BLOCK :] = places.astype(BF)
        leaving.append(pltpu.make_async_copy(built.at[i], out, sent.at[i]))
        leaving[-1].start()
    for c in (*leaving, copies[7]):
        c.wait()


def base_kernel(row, col, tile, count, own, far, dagg, tiles, turned, base, ds, df, ts, ws, dg, sems):
    pieces = [(turned, ws), (own, ds), (far, df), (tiles, ts), (dagg, dg)]
    copies = [pltpu.make_async_copy(a, b, sems.at[i]) for i, (a, b) in enumerate(pieces)]
    for c in copies:
        c.start()
    for c in copies[:3]:
        c.wait()
    blocks = base.shape[0]
    for r in range(2):
        total = wide(ds, df, ws, r, blocks * BLOCK // 2)
        base[r * blocks // 2 : (r + 1) * blocks // 2] = total.reshape(blocks // 2, BLOCK, -1)
    for c in copies[3:]:
        c.wait()
    for s in range(PAIR_MAX):
        j = REACH * PAIR_MAX + s

        @pl.when(live(count, REACH, s))
        def _():
            base[col[0, j]] += dot(ts[tile[0, j]], dg[row[0, j]])


def place_kernel(base, r0, r1, r2, r3, out, token, acc, places):
    token[...] = jnp.zeros_like(token)

    @pl.when(pl.program_id(0) == 0)
    def _():
        for i, r in enumerate((r0, r1, r2, r3)):
            for s in range(PAIR_MAX):
                line = PAIR_MAX * BLOCK + s
                places[i, s] = jnp.max(r[line : line + 1, :].astype(F32)).astype(jnp.int32)

    acc[...] = base[...]
    for i, r in enumerate((r0, r1, r2, r3)):
        for s in range(PAIR_MAX):
            acc[places[i, s]] += r[s * BLOCK : (s + 1) * BLOCK, :].astype(F32)
    out[...] = acc[...].astype(BF)


def assemble_kernel(own_mine, own_swap, far_mine, far_swap, neigh, self_):
    first = lax.axis_index("c") == 0
    side = lax.axis_index("f")
    halves, planes, both, width = own_mine.shape
    piece = both // 2
    own_cols = pl.ds(pl.multiple_of(side * width, 128), width)
    far_cols = pl.ds(pl.multiple_of((1 - side) * width, 128), width)
    for out, a, b in ((neigh, own_mine, own_swap), (self_, own_swap, own_mine)):
        for p in range(planes):
            for h in range(halves):
                n = p * halves + h
                at = slice(n * piece, (n + 1) * piece)
                out[at, own_cols] = jnp.where(first, a[h, p, :piece], b[h, p, :piece]).astype(F32)
    for out, a, b in ((neigh, far_mine, far_swap), (self_, far_swap, far_mine)):
        for n in range(planes * halves):
            at = slice(n * piece, (n + 1) * piece)
            out[at, far_cols] = jnp.where(first, a[n, piece:], b[n, piece:]).astype(F32)


def run(kernel, outs, in_specs, out_specs=None, scratch=(), vmem=16, flops=10**4, **more):
    many = isinstance(outs, list)
    return pl.pallas_call(
        kernel,
        out_shape=outs,
        in_specs=in_specs,
        out_specs=out_specs or ([VMEM] * len(outs) if many else VMEM),
        scratch_shapes=list(scratch),
        compiler_params=params(vmem),
        cost_estimate=pl.CostEstimate(flops=flops, bytes_accessed=10**4, transcendentals=0),
        **more,
    )


def on_device(node_feats, edge_tiles, slot_row, slot_col, slot_tile, slot_count, w_self, w_neigh, bias, cotangent):
    nodes, width = node_feats.shape
    blocks = nodes // BLOCK
    half = width // 2
    scale = float(nodes * lax.axis_size(NODE)) ** (-0.5)
    x = node_feats.reshape(blocks, BLOCK, width)

    ints = (slot_row, slot_col, slot_tile, slot_count)
    wanted = mirror(slot_col, -REACH)
    outer = mirror(x, -1)
    near = swap(x, "c")
    mark = shape((8, 128), F32)
    x_t, neigh_t, self_t, tiles_t, token = run(
        turn_kernel,
        [shape((width, nodes), BF)] + [shape((2 * width, width), BF)] * 2 + [shape(edge_tiles.shape, BF), mark],
        [SMEM] + [VMEM] * 4,
        vmem=20,
    )(wanted, node_feats, w_neigh, w_self, edge_tiles)
    picked = run(
        pick_kernel, shape((PAIR_MAX, BLOCK, width), BF), [SMEM, VMEM, ANY], vmem=4, flops=LONG
    )(wanted, x, token)
    acc0, part, own0, token = run(
        early_kernel,
        [shape((blocks, BLOCK, width), F32)] + [shape((nodes, width), F32)] * 2 + [mark],
        [SMEM] * 4 + [VMEM] * 5 + [ANY],
        vmem=20,
    )(*ints, x, near, edge_tiles, w_self, bias.reshape(1, width), token)

    def after(array, *others, flops=10**4):
        return run(
            pass_kernel,
            shape(array.shape, array.dtype),
            [ANY] * (1 + len(others)),
            ANY,
            input_output_aliases={0: 0},
            vmem=2,
            flops=flops,
        )(array, *others)

    chosen = after(mirror(picked, REACH), flops=LONG)
    outer = after(outer, token)
    passed = swap(outer, "c")
    aggregate, send0, send1 = run(
        aggregate_kernel,
        [shape((nodes, width), BF)] + [shape((nodes, half), BF)] * 2,
        [SMEM] * 4 + [VMEM] * 7,
        scratch=[pltpu.VMEM((blocks, BLOCK, width), F32)],
        vmem=20,
    )(*ints, outer, passed, chosen, acc0, part, edge_tiles, w_neigh)
    recv = [swap(send0, "f"), swap(send1, "f")]

    tall = pl.BlockSpec((TALL, width), lambda i: (i, 0))
    own, agg_t = run(
        own_kernel,
        [shape((nodes, width), F32), shape((width, nodes), BF)],
        [tall, tall, pl.BlockSpec(w_neigh.shape, lambda i: (0, 0))],
        [tall, pl.BlockSpec((width, TALL), lambda i: (0, i))],
        grid=(nodes // TALL,),
    )(aggregate, own0, w_neigh)

    hidden, delta = None, None
    sums = []
    for c in range(2):
        column = pl.BlockSpec((TALL, half), lambda i, c=c: (i, c))
        alone = pl.BlockSpec((TALL, half), lambda i: (i, 0))
        extra = [hidden, delta] if c else []
        hidden, delta, total = run(
            act_kernel,
            [shape((nodes, width), BF), shape((nodes, width), BF), shape((8, half), F32)],
            [column, alone, column] + [ANY] * len(extra),
            [column, column, pl.BlockSpec((8, half), lambda i: (0, 0))],
            grid=(nodes // TALL,),
            input_output_aliases={3: 0, 4: 1} if c else {},
        )(own, recv[c], cotangent, *extra)
        sums.append(total)
    other = after(swap(delta, "f"), flops=LONG)

    plane, chips = lax.axis_size(PLANE), lax.axis_size(CHIPS)
    piece = width // plane
    strip = pl.BlockSpec((width // 2, nodes), lambda i: (i, 0))
    full = pl.BlockSpec((nodes, width), lambda i: (0, 0))
    out = pl.BlockSpec((width // 2, width), lambda i: (i, 0))
    pair = [shape((width, width), BF), shape((width, width), F32)]
    send, keep = run(weight_kernel, pair, [strip, strip, full], [out, out], grid=(2,))(agg_t, x_t, delta)
    got, *got_sums = [swap(v, "c") for v in (send, *sums)]
    steps = 4
    part = pl.BlockSpec((width // steps, width), lambda i: (i, 0))
    small = pl.BlockSpec((8, half), lambda i: (0, 0))
    parts = run(
        join_kernel,
        shape((plane, piece + 8, width), BF),
        [part, part] + [small] * 4,
        pl.BlockSpec((plane // steps, piece + 8, width), lambda i: (i, 0, 0)),
        grid=(steps,),
    )(keep, got, *sums, *got_sums)
    parts = lax.all_to_all(parts, PLANE, 0, 0)

    moved = pl.BlockSpec((plane, piece + 8, width // 2), lambda i: (0, 0, i))
    summed = pl.BlockSpec((piece + 8, width // 2), lambda i: (0, i))
    send, keep, own_total = run(
        weight_total_kernel,
        pair + [shape((piece + 8, width), F32)],
        [strip, strip, full, moved],
        [out, out, summed],
        grid=(2,),
        vmem=50,
    )(agg_t, x_t, other, parts)
    got = swap(send, "c")
    own_got = after(swap(own_total, "xl"), flops=2*10**10)
    parts = run(
        join_kernel,
        shape((chips, width // chips, width), BF),
        [part, part],
        pl.BlockSpec((chips // steps, width // chips, width), lambda i: (i, 0, 0)),
        grid=(steps,),
    )(keep, got)
    far_parts = lax.all_to_all(parts, CHIPS, 0, 0)

    tall_term = PAIR_MAX * BLOCK + 16
    *outward, dagg = run(
        outward_kernel,
        [shape((tall_term, width), BF)] * 4 + [shape((blocks, BLOCK, width), BF)],
        [SMEM] * 4 + [ANY] * 5,
        [ANY] * 5,
        [
            pltpu.VMEM((nodes, width), BF),
            pltpu.VMEM((nodes, width), BF),
            pltpu.VMEM(edge_tiles.shape, BF),
            pltpu.VMEM((2, width, width), BF),
            pltpu.VMEM((blocks, BLOCK, width), BF),
            pltpu.VMEM((nodes, width), F32),
            pltpu.VMEM((4, tall_term, width), BF),
            pltpu.SemaphoreType.DMA((8,)),
            pltpu.SemaphoreType.DMA((4,)),
        ],
        vmem=56,
    )(*ints, delta, other, tiles_t, neigh_t, parts)
    returned = send_roles(outward)

    base = run(
        base_kernel,
        shape((blocks, BLOCK, width), F32),
        [SMEM] * 4 + [ANY] * 5,
        VMEM,
        [
            pltpu.VMEM((nodes, width), BF),
            pltpu.VMEM((nodes, width), BF),
            pltpu.VMEM(edge_tiles.shape, BF),
            pltpu.VMEM(self_t.shape, BF),
            pltpu.VMEM((blocks, BLOCK, width), BF),
            pltpu.SemaphoreType.DMA((5,)),
        ],
        vmem=56,
    )(*ints, delta, other, dagg, tiles_t, self_t)

    spread, grad_bias = run(
        lambda *refs: spread_kernel(scale, *refs),
        [shape((chips, piece, width), BF), shape((1, width), F32)],
        [summed, summed, pl.BlockSpec((chips, width // chips, width // 2), lambda i: (0, 0, i))],
        [
            pl.BlockSpec((chips, piece, width // 2), lambda i: (0, 0, i)),
            pl.BlockSpec((1, width // 2), lambda i: (0, i)),
        ],
        grid=(2,),
    )(own_total, own_got, far_parts)
    column = pl.BlockSpec((blocks, BLOCK, BLOCK), lambda i: (0, 0, i))
    narrow = pl.BlockSpec((tall_term, BLOCK), lambda i: (0, i))
    grad_nodes, token = run(
        place_kernel,
        [shape((blocks, BLOCK, width), BF), mark],
        [column] + [narrow] * 4,
        [column, pl.BlockSpec(mark.shape, lambda i: (0, 0))],
        [pltpu.VMEM((blocks, BLOCK, BLOCK), F32), pltpu.SMEM((4, PAIR_MAX), jnp.int32)],
        grid=(width // BLOCK,),
        vmem=56,
        flops=9*10**9,
    )(base, *returned)
    grad_nodes = grad_nodes.reshape(nodes, width)

    mine = after(lax.all_to_all(spread, CHIPS, 0, 0), token)
    swapped = swap(mine, "c")

    halves = lax.axis_size("xl")
    block = pl.BlockSpec((halves, plane // steps, piece, width), lambda i: (0, i, 0, 0))
    rows = pl.BlockSpec((width // steps, 2 * width), lambda i: (i, 0))
    by_chip = pl.BlockSpec((chips // steps, piece, width), lambda i: (i, 0, 0))
    view = (halves, plane, piece, width)
    grads = run(
        assemble_kernel,
        [shape((width, 2 * width), F32)] * 2,
        [block, block, by_chip, by_chip],
        [rows, rows],
        grid=(steps,),
    )(mine.reshape(view), swapped.reshape(view), mine, swapped)
    grad_neigh, grad_self = grads
    return hidden, grad_nodes, grad_self, grad_neigh, grad_bias.reshape(width)


def solution(mesh):
    fine = Mesh(mesh.devices.reshape(2, 4, 4, 2, 2), (*NODE, "f"))
    placed = (
        P(NODE, "f"),
        P(NODE, None, None),
        P(NODE, None),
        P(NODE, None),
        P(NODE, None),
        P(NODE, None),
        P("f", None),
        P("f", None),
        P("f"),
        P(NODE, "f"),
    )
    return jax.shard_map(
        on_device,
        mesh=fine,
        in_specs=placed,
        out_specs=(P(NODE, "f"), P(NODE, "f"), P("f", None), P("f", None), P("f")),
        check_vma=False,
    )
```

```python
import jax
import jax.numpy as jnp
from jax import lax
from jax.experimental import pallas as pl
from jax.experimental.pallas import tpu as pltpu
from jax.sharding import Mesh, PartitionSpec as P

REACH = 2
PAIR_MAX = 4
BLOCK = 128
NODE = ("xl", "z", "y", "c")
CHIPS = ("xl", "z", "y")
PLANE = ("z", "y")
VMEM = pl.BlockSpec(memory_space=pltpu.VMEM)
SMEM = pl.BlockSpec(memory_space=pltpu.SMEM)
HBM = pl.BlockSpec(memory_space=pltpu.HBM)
ANY = pl.BlockSpec(memory_space=pl.ANY)
BF = jnp.bfloat16
F32 = jnp.float32
MIB = 1 << 20
ROLES = ((4, 0), (0, 4), (1, 3), (3, 1))
TALL = 256
SPLIT = (384, 128)
LONG = 20000000000


def dot(a, b, dims=((1,), (0,))):
    return lax.dot_general(a, b, (dims, ((), ())), preferred_element_type=F32)


def mirror(block, distance):
    count = lax.axis_size(NODE)
    return lax.ppermute(
        block, NODE, [(i, (i + (distance if i % 2 == 0 else -distance)) % count) for i in range(count)]
    )


def swap(block, axis):
    return lax.ppermute(block, axis, [(0, 1), (1, 0)])


def send_roles(blocks):
    ahead, behind, outer, sibling = blocks
    return [mirror(ahead, REACH), mirror(behind, -REACH), mirror(outer, -1), swap(sibling, "c")]


def shape(dims, kind):
    return jax.ShapeDtypeStruct(dims, kind)


def params(vmem):
    return pltpu.CompilerParams(vmem_limit_bytes=vmem * MIB)


def live(count, k, s):
    return s < count[0, k]


def pass_kernel(array, *rest):
    pass


def turn_kernel(wanted, x, w_neigh, w_self, tiles, x_t, neigh_t, self_t, tiles_t, token):
    x_t[...] = x[...].T
    neigh_t[...] = w_neigh[...].T
    self_t[...] = w_self[...].T
    for j in range(tiles.shape[0]):
        tiles_t[j] = tiles[j].T
    token[...] = jnp.zeros_like(token)


def early_kernel(row, col, tile, count, x, near, tiles, w_self, bias, after, acc, ahead, own, token):
    token[...] = jnp.zeros_like(token)
    core = lax.axis_index("c")
    acc[...] = jnp.zeros_like(acc)
    for k, source in ((REACH, x), (jnp.where(core == 0, 3, 1), near)):
        for s in range(PAIR_MAX):
            j = k * PAIR_MAX + s

            @pl.when(live(count, k, s))
            def _():
                acc[row[0, j]] += dot(tiles[tile[0, j]], source[col[0, j]])

    width = own.shape[1]
    side = lax.axis_index("f")
    rows = TALL
    for r in range(own.shape[0] // rows):
        at = slice(r * rows, (r + 1) * rows)
        mine = x[r * rows // BLOCK : (r + 1) * rows // BLOCK].reshape(rows, width)
        ahead[at, :] = dot(mine, w_self[:, pl.ds(pl.multiple_of((1 - side) * width, 128), width)])
        own[at, :] = dot(mine, w_self[:, pl.ds(pl.multiple_of(side * width, 128), width)]) + bias[...]


def pick_kernel(wanted, x, after, out):
    k = jnp.where(lax.axis_index("c") == 0, 0, 4)
    for s in range(PAIR_MAX):
        out[s] = x[wanted[0, k * PAIR_MAX + s]]


def aggregate_kernel(row, col, tile, count, outer, passed, chosen, acc0, part, tiles, w_neigh, agg, send0, send1, acc):
    core = lax.axis_index("c")
    acc[...] = acc0[...]
    for (k0, k1), source in zip(((0, 4), (1, 3), (4, 0)), (chosen, outer, passed)):
        k = jnp.where(core == 0, k0, k1)
        for s in range(PAIR_MAX):
            j = k * PAIR_MAX + s

            @pl.when(live(count, k, s))
            def _():
                block = source[s] if source is chosen else source[col[0, j]]
                acc[row[0, j]] += dot(tiles[tile[0, j]], block)

    rows = acc.shape[0] * BLOCK // 2
    agg[...] = acc[...].astype(BF).reshape(agg.shape)
    start = 0
    other = (1 - lax.axis_index("f")) * agg.shape[1]
    for send in (send0, send1):
        count_of = send.shape[1]
        cols = pl.ds(pl.multiple_of(other + start, 128), count_of)
        span = slice(start, start + count_of)
        for r in range(2):
            at = slice(r * rows, (r + 1) * rows)
            send[at, :] = (dot(agg[at, :], w_neigh[:, cols]) + part[at, span]).astype(BF)
        start += count_of


def own_kernel(agg, own0, w_neigh, out, agg_t):
    width = out.shape[1]
    cols = pl.ds(pl.multiple_of(lax.axis_index("f") * width, 128), width)
    out[...] = dot(agg[...], w_neigh[:, cols]) + own0[...]
    agg_t[...] = agg[...].T


def act_kernel(own, recv, cot, *rest):
    hidden, delta, sums = rest[-3:]
    pre = own[...] + recv[...].astype(F32)
    sigma = jax.nn.sigmoid(pre)
    hidden[...] = (pre * sigma).astype(BF)
    d = (cot[...].astype(F32) * sigma * (1.0 + pre * (1.0 - sigma))).astype(BF)
    delta[...] = d

    @pl.when(pl.program_id(0) == 0)
    def _():
        sums[...] = jnp.zeros_like(sums)

    sums[...] += jnp.sum(d.astype(F32).reshape(-1, 8, d.shape[1]), axis=0)


def weight_kernel(agg_t, x_t, d, *rest):
    send, keep = rest[-2:]
    first = lax.axis_index("c") == 0
    neigh = dot(agg_t[...], d[...])
    own = dot(x_t[...], d[...])
    send[...] = jnp.where(first, own, neigh).astype(BF)
    keep[...] = jnp.where(first, neigh, own)


def weight_total_kernel(agg_t, x_t, d, moved, send, keep, total):
    weight_kernel(agg_t, x_t, d, send, keep)
    total[...] = jnp.sum(moved[...].astype(F32), axis=0)


def bias_rows(sums):
    total = jnp.sum(sums, axis=0, keepdims=True)
    high = total.astype(BF)
    low = (total - high.astype(F32)).astype(BF)
    row = lax.broadcasted_iota(jnp.int32, (8, total.shape[1]), 0)
    return jnp.where(row == 0, high.astype(F32), jnp.where(row == 1, low.astype(F32), 0.0)).astype(BF)


def join_kernel(keep, got, *rest):
    out = rest[-1]
    pieces, tall, width = out.shape
    piece = keep.shape[0] // pieces
    both = (keep[...] + got[...].astype(F32)).astype(BF)
    out[:, :piece, :] = both.reshape(pieces, piece, width)
    if tall > piece:
        s0, s1, g0, g1 = rest[:-1]
        start = 0
        for s, g in ((s0, g0), (s1, g1)):
            rows = bias_rows(jnp.concatenate([s[...], g[...]], axis=0))
            end = start + rows.shape[1]
            out[:, piece:, start:end] = jnp.broadcast_to(rows[None], (pieces, *rows.shape))
            start = end


def spread_kernel(scale, a, b, moved, out, bias):
    piece = out.shape[1] // 2
    xl = lax.axis_index("xl")
    rows = pl.ds(pl.multiple_of(xl * piece, piece), piece)
    mine = (a[rows, :] + b[rows, :]) * scale
    far = jnp.sum(moved[...].astype(F32), axis=0) * scale
    out[:, :piece, :] = jnp.broadcast_to(mine.astype(BF)[None], (out.shape[0], *mine.shape))
    out[:, piece:, :] = jnp.broadcast_to(far.astype(BF)[None], (out.shape[0], *far.shape))
    bias[...] = jnp.sum((a[2 * piece :, :] + b[2 * piece :, :]) * scale, axis=0, keepdims=True)


def wide(own, far, turned, r, rows):
    side = lax.axis_index("f")
    width = own.shape[1]
    at = slice(r * rows, (r + 1) * rows)
    mine = turned[pl.ds(pl.multiple_of(side * width, 128), width), :]
    other = turned[pl.ds(pl.multiple_of((1 - side) * width, 128), width), :]
    return dot(own[at, :], mine) + dot(far[at, :], other)


def outward_kernel(
    row, col, tile, count, own, far, tiles, turned, after,
    o0, o1, o2, o3, dagg, ds, df, ts, wn, dg, total, built, sems, sent,
):
    width = own.shape[1]
    rows = own.shape[0] // 2
    side = lax.axis_index("f")
    copies = []
    for n, (d, held, start) in enumerate(((own, ds, side), (far, df, 1 - side))):
        span = pl.ds(pl.multiple_of(start * width, 128), width)
        copies.append(pltpu.make_async_copy(turned.at[span, :], wn.at[n], sems.at[3 * n]))
        for r in range(2):
            at = pl.ds(r * rows, rows)
            copies.append(pltpu.make_async_copy(d.at[at, :], held.at[at, :], sems.at[3 * n + 1 + r]))
    copies.append(pltpu.make_async_copy(tiles, ts, sems.at[6]))
    copies.append(pltpu.make_async_copy(dg, dagg, sems.at[7]))
    for c in copies[:7]:
        c.start()
    copies[0].wait()
    for r in range(2):
        copies[1 + r].wait()
        at = slice(r * rows, (r + 1) * rows)
        total[at, :] = dot(ds[at, :], wn[0])
    copies[3].wait()
    blocks = dg.shape[0] // 2
    for r in range(2):
        copies[4 + r].wait()
        at = slice(r * rows, (r + 1) * rows)
        both = total[at, :] + dot(df[at, :], wn[1])
        dg[r * blocks : (r + 1) * blocks] = both.astype(BF).reshape(blocks, BLOCK, width)
    copies[7].start()
    copies[6].wait()
    core = lax.axis_index("c")
    leaving = []
    line = lax.broadcasted_iota(jnp.int32, (built.shape[1] - PAIR_MAX * BLOCK, width), 0)
    for i, (out, (k0, k1)) in enumerate(zip((o0, o1, o2, o3), ROLES)):
        k = jnp.where(core == 0, k0, k1)
        places = jnp.zeros(line.shape, F32)
        for s in range(PAIR_MAX):
            j = k * PAIR_MAX + s
            at = slice(s * BLOCK, (s + 1) * BLOCK)

            @pl.when(live(count, k, s))
            def _():
                built[i, at] = dot(ts[tile[0, j]], dg[row[0, j]]).astype(BF)

            @pl.when(jnp.logical_not(live(count, k, s)))
            def _():
                built[i, at] = jnp.zeros((BLOCK, width), BF)

            places = jnp.where(line == s, col[0, j].astype(F32), places)
        built[i, PAIR_MAX * BLOCK :] = places.astype(BF)
        leaving.append(pltpu.make_async_copy(built.at[i], out, sent.at[i]))
        leaving[-1].start()
    for c in (*leaving, copies[7]):
        c.wait()


def base_kernel(row, col, tile, count, own, far, dagg, tiles, turned, base, ds, df, ts, ws, dg, sems):
    pieces = [(turned, ws), (own, ds), (far, df), (tiles, ts), (dagg, dg)]
    copies = [pltpu.make_async_copy(a, b, sems.at[i]) for i, (a, b) in enumerate(pieces)]
    for c in copies:
        c.start()
    for c in copies[:3]:
        c.wait()
    blocks = base.shape[0]
    for r in range(2):
        total = wide(ds, df, ws, r, blocks * BLOCK // 2)
        base[r * blocks // 2 : (r + 1) * blocks // 2] = total.reshape(blocks // 2, BLOCK, -1)
    for c in copies[3:]:
        c.wait()
    for s in range(PAIR_MAX):
        j = REACH * PAIR_MAX + s

        @pl.when(live(count, REACH, s))
        def _():
            base[col[0, j]] += dot(ts[tile[0, j]], dg[row[0, j]])


def place_kernel(base, r0, r1, r2, r3, out, token, acc, places):
    token[...] = jnp.zeros_like(token)

    @pl.when(pl.program_id(0) == 0)
    def _():
        for i, r in enumerate((r0, r1, r2, r3)):
            for s in range(PAIR_MAX):
                line = PAIR_MAX * BLOCK + s
                places[i, s] = jnp.max(r[line : line + 1, :].astype(F32)).astype(jnp.int32)

    acc[...] = base[...]
    for i, r in enumerate((r0, r1, r2, r3)):
        for s in range(PAIR_MAX):
            acc[places[i, s]] += r[s * BLOCK : (s + 1) * BLOCK, :].astype(F32)
    out[...] = acc[...].astype(BF)


def assemble_kernel(own_mine, own_swap, far_mine, far_swap, neigh, self_):
    first = lax.axis_index("c") == 0
    side = lax.axis_index("f")
    halves, planes, both, width = own_mine.shape
    piece = both // 2
    own_cols = pl.ds(pl.multiple_of(side * width, 128), width)
    far_cols = pl.ds(pl.multiple_of((1 - side) * width, 128), width)
    for out, a, b in ((neigh, own_mine, own_swap), (self_, own_swap, own_mine)):
        for p in range(planes):
            for h in range(halves):
                n = p * halves + h
                at = slice(n * piece, (n + 1) * piece)
                out[at, own_cols] = jnp.where(first, a[h, p, :piece], b[h, p, :piece]).astype(F32)
    for out, a, b in ((neigh, far_mine, far_swap), (self_, far_swap, far_mine)):
        for n in range(planes * halves):
            at = slice(n * piece, (n + 1) * piece)
            out[at, far_cols] = jnp.where(first, a[n, piece:], b[n, piece:]).astype(F32)


def run(kernel, outs, in_specs, out_specs=None, scratch=(), vmem=16, flops=10**4, **more):
    many = isinstance(outs, list)
    return pl.pallas_call(
        kernel,
        out_shape=outs,
        in_specs=in_specs,
        out_specs=out_specs or ([VMEM] * len(outs) if many else VMEM),
        scratch_shapes=list(scratch),
        compiler_params=params(vmem),
        cost_estimate=pl.CostEstimate(flops=flops, bytes_accessed=10**4, transcendentals=0),
        **more,
    )


def on_device(node_feats, edge_tiles, slot_row, slot_col, slot_tile, slot_count, w_self, w_neigh, bias, cotangent):
    nodes, width = node_feats.shape
    blocks = nodes // BLOCK
    scale = float(nodes * lax.axis_size(NODE)) ** (-0.5)
    x = node_feats.reshape(blocks, BLOCK, width)

    ints = (slot_row, slot_col, slot_tile, slot_count)
    wanted = mirror(slot_col, -REACH)
    outer = mirror(x, -1)
    near = swap(x, "c")
    mark = shape((8, 128), F32)
    x_t, neigh_t, self_t, tiles_t, token = run(
        turn_kernel,
        [shape((width, nodes), BF)] + [shape((2 * width, width), BF)] * 2 + [shape(edge_tiles.shape, BF), mark],
        [SMEM] + [VMEM] * 4,
        vmem=20,
    )(wanted, node_feats, w_neigh, w_self, edge_tiles)
    picked = run(
        pick_kernel, shape((PAIR_MAX, BLOCK, width), BF), [SMEM, VMEM, ANY], vmem=4, flops=LONG
    )(wanted, x, token)
    acc0, part, own0, token = run(
        early_kernel,
        [shape((blocks, BLOCK, width), F32)] + [shape((nodes, width), F32)] * 2 + [mark],
        [SMEM] * 4 + [VMEM] * 5 + [ANY],
        vmem=20,
    )(*ints, x, near, edge_tiles, w_self, bias.reshape(1, width), token)

    def after(array, *others, flops=10**4):
        return run(
            pass_kernel,
            shape(array.shape, array.dtype),
            [ANY] * (1 + len(others)),
            ANY,
            input_output_aliases={0: 0},
            vmem=2,
            flops=flops,
        )(array, *others)

    chosen = after(mirror(picked, REACH), flops=LONG)
    outer = after(outer, token)
    passed = swap(outer, "c")
    aggregate, send0, send1 = run(
        aggregate_kernel,
        [shape((nodes, width), BF)] + [shape((nodes, n), BF) for n in SPLIT],
        [SMEM] * 4 + [VMEM] * 7,
        scratch=[pltpu.VMEM((blocks, BLOCK, width), F32)],
        vmem=20,
    )(*ints, outer, passed, chosen, acc0, part, edge_tiles, w_neigh)
    recv = [swap(send0, "f"), swap(send1, "f")]

    tall = pl.BlockSpec((TALL, width), lambda i: (i, 0))
    own, agg_t = run(
        own_kernel,
        [shape((nodes, width), F32), shape((width, nodes), BF)],
        [tall, tall, pl.BlockSpec(w_neigh.shape, lambda i: (0, 0))],
        [tall, pl.BlockSpec((width, TALL), lambda i: (0, i))],
        grid=(nodes // TALL,),
    )(aggregate, own0, w_neigh)

    hidden, delta = None, None
    sums = []
    for c in range(2):
        narrow = SPLIT[c]
        rows = (1 + c) * TALL
        column = pl.BlockSpec((rows, narrow), lambda i, at=c * SPLIT[0] // narrow: (i, at))
        alone = pl.BlockSpec((rows, narrow), lambda i: (i, 0))
        extra = [hidden, delta] if c else []
        hidden, delta, total = run(
            act_kernel,
            [shape((nodes, width), BF), shape((nodes, width), BF), shape((8, narrow), F32)],
            [column, alone, column] + [ANY] * len(extra),
            [column, column, pl.BlockSpec((8, narrow), lambda i: (0, 0))],
            grid=(nodes // rows,),
            input_output_aliases={3: 0, 4: 1} if c else {},
        )(own, recv[c], cotangent, *extra)
        sums.append(total)
    other = after(swap(delta, "f"), flops=LONG)

    plane, chips = lax.axis_size(PLANE), lax.axis_size(CHIPS)
    piece = width // plane
    strip = pl.BlockSpec((width // 2, nodes), lambda i: (i, 0))
    full = pl.BlockSpec((nodes, width), lambda i: (0, 0))
    out = pl.BlockSpec((width // 2, width), lambda i: (i, 0))
    pair = [shape((width, width), BF), shape((width, width), F32)]
    send, keep = run(weight_kernel, pair, [strip, strip, full], [out, out], grid=(2,))(agg_t, x_t, delta)
    got, *got_sums = [swap(v, "c") for v in (send, *sums)]
    steps = 2
    part = pl.BlockSpec((width // steps, width), lambda i: (i, 0))
    small = [pl.BlockSpec((8, n), lambda i: (0, 0)) for n in SPLIT]
    parts = run(
        join_kernel,
        shape((plane, piece + 8, width), BF),
        [part, part] + small * 2,
        pl.BlockSpec((plane // steps, piece + 8, width), lambda i: (i, 0, 0)),
        grid=(steps,),
    )(keep, got, *sums, *got_sums)
    parts = lax.all_to_all(parts, PLANE, 0, 0)

    moved = pl.BlockSpec((plane, piece + 8, width // 2), lambda i: (0, 0, i))
    summed = pl.BlockSpec((piece + 8, width // 2), lambda i: (0, i))
    send, keep, own_total = run(
        weight_total_kernel,
        pair + [shape((piece + 8, width), F32)],
        [strip, strip, full, moved],
        [out, out, summed],
        grid=(2,),
        vmem=50,
    )(agg_t, x_t, other, parts)
    got = swap(send, "c")
    own_got = after(swap(own_total, "xl"), flops=2*10**10)
    parts = run(
        join_kernel,
        shape((chips, width // chips, width), BF),
        [part, part],
        pl.BlockSpec((chips // steps, width // chips, width), lambda i: (i, 0, 0)),
        grid=(steps,),
    )(keep, got)
    far_parts = lax.all_to_all(parts, CHIPS, 0, 0)

    tall_term = PAIR_MAX * BLOCK + 16
    *outward, dagg = run(
        outward_kernel,
        [shape((tall_term, width), BF)] * 4 + [shape((blocks, BLOCK, width), BF)],
        [SMEM] * 4 + [ANY] * 5,
        [ANY] * 5,
        [
            pltpu.VMEM((nodes, width), BF),
            pltpu.VMEM((nodes, width), BF),
            pltpu.VMEM(edge_tiles.shape, BF),
            pltpu.VMEM((2, width, width), BF),
            pltpu.VMEM((blocks, BLOCK, width), BF),
            pltpu.VMEM((nodes, width), F32),
            pltpu.VMEM((4, tall_term, width), BF),
            pltpu.SemaphoreType.DMA((8,)),
            pltpu.SemaphoreType.DMA((4,)),
        ],
        vmem=56,
    )(*ints, delta, other, tiles_t, neigh_t, parts)
    returned = send_roles(outward)

    base = run(
        base_kernel,
        shape((blocks, BLOCK, width), F32),
        [SMEM] * 4 + [ANY] * 5,
        VMEM,
        [
            pltpu.VMEM((nodes, width), BF),
            pltpu.VMEM((nodes, width), BF),
            pltpu.VMEM(edge_tiles.shape, BF),
            pltpu.VMEM(self_t.shape, BF),
            pltpu.VMEM((blocks, BLOCK, width), BF),
            pltpu.SemaphoreType.DMA((5,)),
        ],
        vmem=56,
    )(*ints, delta, other, dagg, tiles_t, self_t)

    spread, grad_bias = run(
        lambda *refs: spread_kernel(scale, *refs),
        [shape((chips, piece, width), BF), shape((1, width), F32)],
        [summed, summed, pl.BlockSpec((chips, width // chips, width // 2), lambda i: (0, 0, i))],
        [
            pl.BlockSpec((chips, piece, width // 2), lambda i: (0, 0, i)),
            pl.BlockSpec((1, width // 2), lambda i: (0, i)),
        ],
        grid=(2,),
    )(own_total, own_got, far_parts)
    lanes = 2 * BLOCK
    column = pl.BlockSpec((blocks, BLOCK, lanes), lambda i: (0, 0, i))
    narrow = pl.BlockSpec((tall_term, lanes), lambda i: (0, i))
    grad_nodes, token = run(
        place_kernel,
        [shape((blocks, BLOCK, width), BF), mark],
        [column] + [narrow] * 4,
        [column, pl.BlockSpec(mark.shape, lambda i: (0, 0))],
        [pltpu.VMEM((blocks, BLOCK, lanes), F32), pltpu.SMEM((4, PAIR_MAX), jnp.int32)],
        grid=(width // lanes,),
        vmem=56,
        flops=9*10**9,
    )(base, *returned)
    grad_nodes = grad_nodes.reshape(nodes, width)

    mine = after(lax.all_to_all(spread, CHIPS, 0, 0), token)
    swapped = swap(mine, "c")

    halves = lax.axis_size("xl")
    block = pl.BlockSpec((halves, plane // steps, piece, width), lambda i: (0, i, 0, 0))
    rows = pl.BlockSpec((width // steps, 2 * width), lambda i: (i, 0))
    by_chip = pl.BlockSpec((chips // steps, piece, width), lambda i: (i, 0, 0))
    view = (halves, plane, piece, width)
    grads = run(
        assemble_kernel,
        [shape((width, 2 * width), F32)] * 2,
        [block, block, by_chip, by_chip],
        [rows, rows],
        grid=(steps,),
    )(mine.reshape(view), swapped.reshape(view), mine, swapped)
    grad_neigh, grad_self = grads
    return hidden, grad_nodes, grad_self, grad_neigh, grad_bias.reshape(width)


def solution(mesh):
    fine = Mesh(mesh.devices.reshape(2, 4, 4, 2, 2), (*NODE, "f"))
    placed = (
        P(NODE, "f"),
        P(NODE, None, None),
        P(NODE, None),
        P(NODE, None),
        P(NODE, None),
        P(NODE, None),
        P("f", None),
        P("f", None),
        P("f"),
        P(NODE, "f"),
    )
    return jax.shard_map(
        on_device,
        mesh=fine,
        in_specs=placed,
        out_specs=(P(NODE, "f"), P(NODE, "f"), P("f", None), P("f", None), P("f")),
        check_vma=False,
    )
```

```python
import jax
import jax.numpy as jnp
from jax import lax
from jax.experimental import pallas as pl
from jax.experimental.pallas import tpu as pltpu
from jax.sharding import Mesh, PartitionSpec as P

REACH = 2
PAIR_MAX = 4
BLOCK = 128
NODE = ("xl", "z", "y", "c")
CHIPS = ("xl", "z", "y")
PLANE = ("z", "y")
VMEM = pl.BlockSpec(memory_space=pltpu.VMEM)
SMEM = pl.BlockSpec(memory_space=pltpu.SMEM)
HBM = pl.BlockSpec(memory_space=pltpu.HBM)
ANY = pl.BlockSpec(memory_space=pl.ANY)
BF = jnp.bfloat16
F32 = jnp.float32
MIB = 1 << 20
ROLES = ((4, 0), (0, 4), (1, 3), (3, 1))
TALL = 256
SPLIT = (256, 256)
LONG = 20000000000


def dot(a, b, dims=((1,), (0,))):
    return lax.dot_general(a, b, (dims, ((), ())), preferred_element_type=F32)


def mirror(block, distance):
    count = lax.axis_size(NODE)
    return lax.ppermute(
        block, NODE, [(i, (i + (distance if i % 2 == 0 else -distance)) % count) for i in range(count)]
    )


def swap(block, axis):
    return lax.ppermute(block, axis, [(0, 1), (1, 0)])


def send_roles(blocks):
    ahead, behind, outer, sibling = blocks
    return [mirror(ahead, REACH), mirror(behind, -REACH), mirror(outer, -1), swap(sibling, "c")]


def shape(dims, kind):
    return jax.ShapeDtypeStruct(dims, kind)


def params(vmem):
    return pltpu.CompilerParams(vmem_limit_bytes=vmem * MIB)


def live(count, k, s):
    return s < count[0, k]


def pass_kernel(array, *rest):
    pass


def turn_kernel(wanted, x, w_neigh, w_self, tiles, x_t, neigh_t, self_t, tiles_t, token):
    x_t[...] = x[...].T
    neigh_t[...] = w_neigh[...].T
    self_t[...] = w_self[...].T
    for j in range(tiles.shape[0]):
        tiles_t[j] = tiles[j].T
    token[...] = jnp.zeros_like(token)


def early_kernel(row, col, tile, count, x, near, tiles, w_self, bias, after, acc, ahead, own, token):
    token[...] = jnp.zeros_like(token)
    core = lax.axis_index("c")
    acc[...] = jnp.zeros_like(acc)
    for k, source in ((REACH, x), (jnp.where(core == 0, 3, 1), near)):
        for s in range(PAIR_MAX):
            j = k * PAIR_MAX + s

            @pl.when(live(count, k, s))
            def _():
                acc[row[0, j]] += dot(tiles[tile[0, j]], source[col[0, j]])

    width = own.shape[1]
    side = lax.axis_index("f")
    rows = TALL
    for r in range(own.shape[0] // rows):
        at = slice(r * rows, (r + 1) * rows)
        mine = x[r * rows // BLOCK : (r + 1) * rows // BLOCK].reshape(rows, width)
        ahead[at, :] = dot(mine, w_self[:, pl.ds(pl.multiple_of((1 - side) * width, 128), width)])
        own[at, :] = dot(mine, w_self[:, pl.ds(pl.multiple_of(side * width, 128), width)]) + bias[...]


def pick_kernel(wanted, x, after, out):
    k = jnp.where(lax.axis_index("c") == 0, 0, 4)
    for s in range(PAIR_MAX):
        out[s] = x[wanted[0, k * PAIR_MAX + s]]


def aggregate_kernel(row, col, tile, count, outer, passed, chosen, acc0, part, tiles, w_neigh, agg, send0, send1, acc):
    core = lax.axis_index("c")
    acc[...] = acc0[...]
    for (k0, k1), source in zip(((0, 4), (1, 3), (4, 0)), (chosen, outer, passed)):
        k = jnp.where(core == 0, k0, k1)
        for s in range(PAIR_MAX):
            j = k * PAIR_MAX + s

            @pl.when(live(count, k, s))
            def _():
                block = source[s] if source is chosen else source[col[0, j]]
                acc[row[0, j]] += dot(tiles[tile[0, j]], block)

    rows = acc.shape[0] * BLOCK // 2
    agg[...] = acc[...].astype(BF).reshape(agg.shape)
    start = 0
    other = (1 - lax.axis_index("f")) * agg.shape[1]
    for send in (send0, send1):
        count_of = send.shape[1]
        cols = pl.ds(pl.multiple_of(other + start, 128), count_of)
        span = slice(start, start + count_of)
        for r in range(2):
            at = slice(r * rows, (r + 1) * rows)
            send[at, :] = (dot(agg[at, :], w_neigh[:, cols]) + part[at, span]).astype(BF)
        start += count_of


def own_kernel(agg, own0, w_neigh, out, agg_t):
    width = out.shape[1]
    cols = pl.ds(pl.multiple_of(lax.axis_index("f") * width, 128), width)
    out[...] = dot(agg[...], w_neigh[:, cols]) + own0[...]
    agg_t[...] = agg[...].T


def act_kernel(own, recv, cot, *rest):
    hidden, delta, sums = rest[-3:]
    pre = own[...] + recv[...].astype(F32)
    sigma = jax.nn.sigmoid(pre)
    hidden[...] = (pre * sigma).astype(BF)
    d = (cot[...].astype(F32) * sigma * (1.0 + pre * (1.0 - sigma))).astype(BF)
    delta[...] = d

    @pl.when(pl.program_id(0) == 0)
    def _():
        sums[...] = jnp.zeros_like(sums)

    sums[...] += jnp.sum(d.astype(F32).reshape(-1, 8, d.shape[1]), axis=0)


def weight_kernel(agg_t, x_t, d, *rest):
    send, keep = rest[-2:]
    first = lax.axis_index("c") == 0
    neigh = dot(agg_t[...], d[...])
    own = dot(x_t[...], d[...])
    send[...] = jnp.where(first, own, neigh).astype(BF)
    keep[...] = jnp.where(first, neigh, own)


def weight_total_kernel(agg_t, x_t, d, moved, send, keep, total):
    weight_kernel(agg_t, x_t, d, send, keep)
    total[...] = jnp.sum(moved[...].astype(F32), axis=0)


def bias_rows(sums):
    total = jnp.sum(sums, axis=0, keepdims=True)
    high = total.astype(BF)
    low = (total - high.astype(F32)).astype(BF)
    row = lax.broadcasted_iota(jnp.int32, (8, total.shape[1]), 0)
    return jnp.where(row == 0, high.astype(F32), jnp.where(row == 1, low.astype(F32), 0.0)).astype(BF)


def join_kernel(keep, got, *rest):
    out = rest[-1]
    pieces, tall, width = out.shape
    piece = keep.shape[0] // pieces
    both = (keep[...] + got[...].astype(F32)).astype(BF)
    out[:, :piece, :] = both.reshape(pieces, piece, width)
    if tall > piece:
        s0, s1, g0, g1 = rest[:-1]
        start = 0
        for s, g in ((s0, g0), (s1, g1)):
            rows = bias_rows(jnp.concatenate([s[...], g[...]], axis=0))
            end = start + rows.shape[1]
            out[:, piece:, start:end] = jnp.broadcast_to(rows[None], (pieces, *rows.shape))
            start = end


def spread_kernel(scale, a, b, moved, out, bias):
    piece = out.shape[1] // 2
    xl = lax.axis_index("xl")
    rows = pl.ds(pl.multiple_of(xl * piece, piece), piece)
    mine = (a[rows, :] + b[rows, :]) * scale
    far = jnp.sum(moved[...].astype(F32), axis=0) * scale
    out[:, :piece, :] = jnp.broadcast_to(mine.astype(BF)[None], (out.shape[0], *mine.shape))
    out[:, piece:, :] = jnp.broadcast_to(far.astype(BF)[None], (out.shape[0], *far.shape))
    bias[...] = jnp.sum((a[2 * piece :, :] + b[2 * piece :, :]) * scale, axis=0, keepdims=True)


def wide(own, far, turned, r, rows):
    side = lax.axis_index("f")
    width = own.shape[1]
    at = slice(r * rows, (r + 1) * rows)
    mine = turned[pl.ds(pl.multiple_of(side * width, 128), width), :]
    other = turned[pl.ds(pl.multiple_of((1 - side) * width, 128), width), :]
    return dot(own[at, :], mine) + dot(far[at, :], other)


def outward_kernel(
    row, col, tile, count, own, far, tiles, turned, after,
    o0, o1, o2, o3, dagg, ds, df, ts, wn, dg, total, built, sems, sent,
):
    width = own.shape[1]
    rows = own.shape[0] // 2
    side = lax.axis_index("f")
    copies = []
    for n, (d, held, start) in enumerate(((own, ds, side), (far, df, 1 - side))):
        span = pl.ds(pl.multiple_of(start * width, 128), width)
        copies.append(pltpu.make_async_copy(turned.at[span, :], wn.at[n], sems.at[3 * n]))
        for r in range(2):
            at = pl.ds(r * rows, rows)
            copies.append(pltpu.make_async_copy(d.at[at, :], held.at[at, :], sems.at[3 * n + 1 + r]))
    copies.append(pltpu.make_async_copy(tiles, ts, sems.at[6]))
    copies.append(pltpu.make_async_copy(dg, dagg, sems.at[7]))
    for c in copies[:7]:
        c.start()
    copies[0].wait()
    for r in range(2):
        copies[1 + r].wait()
        at = slice(r * rows, (r + 1) * rows)
        total[at, :] = dot(ds[at, :], wn[0])
    copies[3].wait()
    blocks = dg.shape[0] // 2
    for r in range(2):
        copies[4 + r].wait()
        at = slice(r * rows, (r + 1) * rows)
        both = total[at, :] + dot(df[at, :], wn[1])
        dg[r * blocks : (r + 1) * blocks] = both.astype(BF).reshape(blocks, BLOCK, width)
    copies[7].start()
    copies[6].wait()
    core = lax.axis_index("c")
    leaving = []
    line = lax.broadcasted_iota(jnp.int32, (built.shape[1] - PAIR_MAX * BLOCK, width), 0)
    for i, (out, (k0, k1)) in enumerate(zip((o0, o1, o2, o3), ROLES)):
        k = jnp.where(core == 0, k0, k1)
        places = jnp.zeros(line.shape, F32)
        for s in range(PAIR_MAX):
            j = k * PAIR_MAX + s
            at = slice(s * BLOCK, (s + 1) * BLOCK)

            @pl.when(live(count, k, s))
            def _():
                built[i, at] = dot(ts[tile[0, j]], dg[row[0, j]]).astype(BF)

            @pl.when(jnp.logical_not(live(count, k, s)))
            def _():
                built[i, at] = jnp.zeros((BLOCK, width), BF)

            places = jnp.where(line == s, col[0, j].astype(F32), places)
        built[i, PAIR_MAX * BLOCK :] = places.astype(BF)
        leaving.append(pltpu.make_async_copy(built.at[i], out, sent.at[i]))
        leaving[-1].start()
    for c in (*leaving, copies[7]):
        c.wait()


def base_kernel(row, col, tile, count, own, far, dagg, tiles, turned, base, ds, df, ts, ws, dg, sems):
    pieces = [(turned, ws), (own, ds), (far, df), (tiles, ts), (dagg, dg)]
    copies = [pltpu.make_async_copy(a, b, sems.at[i]) for i, (a, b) in enumerate(pieces)]
    for c in copies:
        c.start()
    for c in copies[:3]:
        c.wait()
    blocks = base.shape[0]
    for r in range(2):
        total = wide(ds, df, ws, r, blocks * BLOCK // 2)
        base[r * blocks // 2 : (r + 1) * blocks // 2] = total.reshape(blocks // 2, BLOCK, -1)
    for c in copies[3:]:
        c.wait()
    for s in range(PAIR_MAX):
        j = REACH * PAIR_MAX + s

        @pl.when(live(count, REACH, s))
        def _():
            base[col[0, j]] += dot(ts[tile[0, j]], dg[row[0, j]])


def place_kernel(base, r0, r1, r2, r3, out, token, acc, places):
    token[...] = jnp.zeros_like(token)

    @pl.when(pl.program_id(0) == 0)
    def _():
        for i, r in enumerate((r0, r1, r2, r3)):
            for s in range(PAIR_MAX):
                line = PAIR_MAX * BLOCK + s
                places[i, s] = jnp.max(r[line : line + 1, :].astype(F32)).astype(jnp.int32)

    acc[...] = base[...]
    for i, r in enumerate((r0, r1, r2, r3)):
        for s in range(PAIR_MAX):
            acc[places[i, s]] += r[s * BLOCK : (s + 1) * BLOCK, :].astype(F32)
    out[...] = acc[...].astype(BF)


def assemble_kernel(own_mine, own_swap, far_mine, far_swap, neigh, self_):
    first = lax.axis_index("c") == 0
    side = lax.axis_index("f")
    halves, planes, both, width = own_mine.shape
    piece = both // 2
    own_cols = pl.ds(pl.multiple_of(side * width, 128), width)
    far_cols = pl.ds(pl.multiple_of((1 - side) * width, 128), width)
    for out, a, b in ((neigh, own_mine, own_swap), (self_, own_swap, own_mine)):
        for p in range(planes):
            for h in range(halves):
                n = p * halves + h
                at = slice(n * piece, (n + 1) * piece)
                out[at, own_cols] = jnp.where(first, a[h, p, :piece], b[h, p, :piece]).astype(F32)
    for out, a, b in ((neigh, far_mine, far_swap), (self_, far_swap, far_mine)):
        for n in range(planes * halves):
            at = slice(n * piece, (n + 1) * piece)
            out[at, far_cols] = jnp.where(first, a[n, piece:], b[n, piece:]).astype(F32)


def run(kernel, outs, in_specs, out_specs=None, scratch=(), vmem=16, flops=10**4, **more):
    many = isinstance(outs, list)
    return pl.pallas_call(
        kernel,
        out_shape=outs,
        in_specs=in_specs,
        out_specs=out_specs or ([VMEM] * len(outs) if many else VMEM),
        scratch_shapes=list(scratch),
        compiler_params=params(vmem),
        cost_estimate=pl.CostEstimate(flops=flops, bytes_accessed=10**4, transcendentals=0),
        **more,
    )


def on_device(node_feats, edge_tiles, slot_row, slot_col, slot_tile, slot_count, w_self, w_neigh, bias, cotangent):
    nodes, width = node_feats.shape
    blocks = nodes // BLOCK
    scale = float(nodes * lax.axis_size(NODE)) ** (-0.5)
    x = node_feats.reshape(blocks, BLOCK, width)

    ints = (slot_row, slot_col, slot_tile, slot_count)
    wanted = mirror(slot_col, -REACH)
    outer = mirror(x, -1)
    near = swap(x, "c")
    mark = shape((8, 128), F32)
    x_t, neigh_t, self_t, tiles_t, token = run(
        turn_kernel,
        [shape((width, nodes), BF)] + [shape((2 * width, width), BF)] * 2 + [shape(edge_tiles.shape, BF), mark],
        [SMEM] + [VMEM] * 4,
        vmem=20,
    )(wanted, node_feats, w_neigh, w_self, edge_tiles)
    picked = run(
        pick_kernel, shape((PAIR_MAX, BLOCK, width), BF), [SMEM, VMEM, ANY], vmem=4, flops=LONG
    )(wanted, x, token)
    acc0, part, own0, token = run(
        early_kernel,
        [shape((blocks, BLOCK, width), F32)] + [shape((nodes, width), F32)] * 2 + [mark],
        [SMEM] * 4 + [VMEM] * 5 + [ANY],
        vmem=20,
    )(*ints, x, near, edge_tiles, w_self, bias.reshape(1, width), token)

    def after(array, *others, flops=10**4):
        return run(
            pass_kernel,
            shape(array.shape, array.dtype),
            [ANY] * (1 + len(others)),
            ANY,
            input_output_aliases={0: 0},
            vmem=2,
            flops=flops,
        )(array, *others)

    chosen = after(mirror(picked, REACH), flops=LONG)
    outer = after(outer, token)
    passed = swap(outer, "c")
    aggregate, send0, send1 = run(
        aggregate_kernel,
        [shape((nodes, width), BF)] + [shape((nodes, n), BF) for n in SPLIT],
        [SMEM] * 4 + [VMEM] * 7,
        scratch=[pltpu.VMEM((blocks, BLOCK, width), F32)],
        vmem=20,
    )(*ints, outer, passed, chosen, acc0, part, edge_tiles, w_neigh)
    recv = [swap(send0, "f"), swap(send1, "f")]

    tall = pl.BlockSpec((TALL, width), lambda i: (i, 0))
    own, agg_t = run(
        own_kernel,
        [shape((nodes, width), F32), shape((width, nodes), BF)],
        [tall, tall, pl.BlockSpec(w_neigh.shape, lambda i: (0, 0))],
        [tall, pl.BlockSpec((width, TALL), lambda i: (0, i))],
        grid=(nodes // TALL,),
    )(aggregate, own0, w_neigh)

    hidden, delta = None, None
    sums = []
    for c in range(2):
        narrow = SPLIT[c]
        rows = (1 + c) * TALL
        column = pl.BlockSpec((rows, narrow), lambda i, at=c * SPLIT[0] // narrow: (i, at))
        alone = pl.BlockSpec((rows, narrow), lambda i: (i, 0))
        extra = [hidden, delta] if c else []
        hidden, delta, total = run(
            act_kernel,
            [shape((nodes, width), BF), shape((nodes, width), BF), shape((8, narrow), F32)],
            [column, alone, column] + [ANY] * len(extra),
            [column, column, pl.BlockSpec((8, narrow), lambda i: (0, 0))],
            grid=(nodes // rows,),
            input_output_aliases={3: 0, 4: 1} if c else {},
        )(own, recv[c], cotangent, *extra)
        sums.append(total)
    other = after(swap(delta, "f"), flops=LONG)

    plane, chips = lax.axis_size(PLANE), lax.axis_size(CHIPS)
    piece = width // plane
    strip = pl.BlockSpec((width // 2, nodes), lambda i: (i, 0))
    full = pl.BlockSpec((nodes, width), lambda i: (0, 0))
    out = pl.BlockSpec((width // 2, width), lambda i: (i, 0))
    pair = [shape((width, width), BF), shape((width, width), F32)]
    send, keep = run(weight_kernel, pair, [strip, strip, full], [out, out], grid=(2,))(agg_t, x_t, delta)
    got, *got_sums = [swap(v, "c") for v in (send, *sums)]
    steps = 2
    part = pl.BlockSpec((width // steps, width), lambda i: (i, 0))
    small = [pl.BlockSpec((8, n), lambda i: (0, 0)) for n in SPLIT]
    parts = run(
        join_kernel,
        shape((plane, piece + 8, width), BF),
        [part, part] + small * 2,
        pl.BlockSpec((plane // steps, piece + 8, width), lambda i: (i, 0, 0)),
        grid=(steps,),
    )(keep, got, *sums, *got_sums)
    parts = lax.all_to_all(parts, PLANE, 0, 0)

    moved = pl.BlockSpec((plane, piece + 8, width // 2), lambda i: (0, 0, i))
    summed = pl.BlockSpec((piece + 8, width // 2), lambda i: (0, i))
    send, keep, own_total = run(
        weight_total_kernel,
        pair + [shape((piece + 8, width), F32)],
        [strip, strip, full, moved],
        [out, out, summed],
        grid=(2,),
        vmem=50,
    )(agg_t, x_t, other, parts)
    got = swap(send, "c")
    own_got = after(swap(own_total, "xl"), flops=2*10**10)
    parts = run(
        join_kernel,
        shape((chips, width // chips, width), BF),
        [part, part],
        pl.BlockSpec((chips // steps, width // chips, width), lambda i: (i, 0, 0)),
        grid=(steps,),
    )(keep, got)
    far_parts = lax.all_to_all(parts, CHIPS, 0, 0)

    tall_term = PAIR_MAX * BLOCK + 16
    *outward, dagg = run(
        outward_kernel,
        [shape((tall_term, width), BF)] * 4 + [shape((blocks, BLOCK, width), BF)],
        [SMEM] * 4 + [ANY] * 5,
        [ANY] * 5,
        [
            pltpu.VMEM((nodes, width), BF),
            pltpu.VMEM((nodes, width), BF),
            pltpu.VMEM(edge_tiles.shape, BF),
            pltpu.VMEM((2, width, width), BF),
            pltpu.VMEM((blocks, BLOCK, width), BF),
            pltpu.VMEM((nodes, width), F32),
            pltpu.VMEM((4, tall_term, width), BF),
            pltpu.SemaphoreType.DMA((8,)),
            pltpu.SemaphoreType.DMA((4,)),
        ],
        vmem=56,
    )(*ints, delta, other, tiles_t, neigh_t, parts)
    returned = send_roles(outward)

    base = run(
        base_kernel,
        shape((blocks, BLOCK, width), F32),
        [SMEM] * 4 + [ANY] * 5,
        VMEM,
        [
            pltpu.VMEM((nodes, width), BF),
            pltpu.VMEM((nodes, width), BF),
            pltpu.VMEM(edge_tiles.shape, BF),
            pltpu.VMEM(self_t.shape, BF),
            pltpu.VMEM((blocks, BLOCK, width), BF),
            pltpu.SemaphoreType.DMA((5,)),
        ],
        vmem=56,
    )(*ints, delta, other, dagg, tiles_t, self_t)

    spread, grad_bias = run(
        lambda *refs: spread_kernel(scale, *refs),
        [shape((chips, piece, width), BF), shape((1, width), F32)],
        [VMEM] * 3,
    )(own_total, own_got, far_parts)
    lanes = 2 * BLOCK
    column = pl.BlockSpec((blocks, BLOCK, lanes), lambda i: (0, 0, i))
    narrow = pl.BlockSpec((tall_term, lanes), lambda i: (0, i))
    grad_nodes, token = run(
        place_kernel,
        [shape((blocks, BLOCK, width), BF), mark],
        [column] + [narrow] * 4,
        [column, pl.BlockSpec(mark.shape, lambda i: (0, 0))],
        [pltpu.VMEM((blocks, BLOCK, lanes), F32), pltpu.SMEM((4, PAIR_MAX), jnp.int32)],
        grid=(width // lanes,),
        vmem=56,
        flops=9*10**9,
    )(base, *returned)
    grad_nodes = grad_nodes.reshape(nodes, width)

    mine = after(lax.all_to_all(spread, CHIPS, 0, 0), token)
    swapped = swap(mine, "c")

    halves = lax.axis_size("xl")
    block = pl.BlockSpec((halves, plane // steps, piece, width), lambda i: (0, i, 0, 0))
    rows = pl.BlockSpec((width // steps, 2 * width), lambda i: (i, 0))
    by_chip = pl.BlockSpec((chips // steps, piece, width), lambda i: (i, 0, 0))
    view = (halves, plane, piece, width)
    grads = run(
        assemble_kernel,
        [shape((width, 2 * width), F32)] * 2,
        [block, block, by_chip, by_chip],
        [rows, rows],
        grid=(steps,),
    )(mine.reshape(view), swapped.reshape(view), mine, swapped)
    grad_neigh, grad_self = grads
    return hidden, grad_nodes, grad_self, grad_neigh, grad_bias.reshape(width)


def solution(mesh):
    fine = Mesh(mesh.devices.reshape(2, 4, 4, 2, 2), (*NODE, "f"))
    placed = (
        P(NODE, "f"),
        P(NODE, None, None),
        P(NODE, None),
        P(NODE, None),
        P(NODE, None),
        P(NODE, None),
        P("f", None),
        P("f", None),
        P("f"),
        P(NODE, "f"),
    )
    return jax.shard_map(
        on_device,
        mesh=fine,
        in_specs=placed,
        out_specs=(P(NODE, "f"), P(NODE, "f"), P("f", None), P("f", None), P("f")),
        check_vma=False,
    )
```
